512 devices in a mesh: expert: 128 (over z, y, core), pair: 4 (over x).
Axes of the slice: x: 4, y: 8, z: 8, core: 2. Of those that a mesh axis runs over, the one named last changes fastest.
Arguments:
- tokens: bfloat16 [2048, 4096], P('expert', 'pair'), may hold values from -6 to 6
- routes: int32 [2048, 8], P('expert'), may hold values from 0 to 127, as said below
- router_probs: float32 [2048, 8], P('expert'), may hold values from 0.02 to 1
- w_gate: bfloat16 [128, 768, 4096], P('expert', 'pair'), may hold values from -0.09375 to 0.09375
- w_up: bfloat16 [128, 768, 4096], P('expert', 'pair'), may hold values from -0.09375 to 0.09375
- w_down: bfloat16 [128, 768, 4096], P('expert', 'pair'), may hold values from -0.4375 to 0.4375
Outputs:
- expert_mix: bfloat16 [2048, 4096], P('expert', 'pair')
The draws below stay inside these ranges and needn't reach their ends.
Inputs may be any that keep to these rules, and one draw needn't show every extreme that they name: `routes`: each row names 8 different experts. In every aligned block of 16 rows (one index of expert's micro-batch; micro-batch m of that index is its rows m * 16 to (m + 1) * 16 - 1), exactly half of the 128 experts are named, each by exactly 2 rows.
All inputs are finite; a program needn't handle non-finite values.
Results may differ from the reference program's by a relative error of at most 0.017.
Values may be sent and summed in bfloat16 or wider, within the bound.
A program may use at most 64 MiB of HBM per device.

```python
import math
import jax
import jax.numpy as jnp
from jax import lax

D = 4096
FF = 768
TOP = 8
TOK_MB = 16
MICRO = 1
EXPERTS = 128
TOKENS = 2048
CAP = 2
N_EXPERT = 128
N_PAIR = 4


def draw_routes(key, part):
    blocks = TOKENS // TOK_MB
    chosen = EXPERTS // 2
    stride = chosen // TOK_MB
    key_tier = jax.random.fold_in(key, 11)
    key_hot = jax.random.fold_in(key, 12)
    key_noise = jax.random.fold_in(key, 13)
    key_order = jax.random.fold_in(key, 14)
    tier = jax.random.randint(key_tier, (EXPERTS,), 0, 4) * 4096
    hot = jax.random.randint(key_hot, (MICRO,), 0, EXPERTS)
    noise = jax.random.randint(key_noise, (blocks, EXPERTS), 0, 4096)
    micro_of = jnp.arange(blocks) % MICRO
    hot_mark = (jnp.arange(EXPERTS)[None, :] == hot[micro_of][:, None]).astype(jnp.int32) * 65536
    expert_ids = jnp.arange(EXPERTS, dtype=jnp.int32)
    ends = jnp.logical_or(expert_ids == 0, expert_ids == EXPERTS - 1)
    first_block = jnp.arange(blocks) == 0
    end_mark = jnp.logical_and(first_block[:, None], ends[None, :]).astype(jnp.int32) * 131072
    scores = (noise + tier[None, :] + hot_mark + end_mark) * EXPERTS + expert_ids[None, :]
    _, selected = lax.top_k(scores, chosen)
    order_keys = jax.random.randint(key_order, (blocks, chosen), 0, 65536) * chosen + jnp.arange(chosen, dtype=jnp.int32)[None, :]
    order = jnp.argsort(order_keys, axis=1)
    shuffled = jnp.take_along_axis(selected, order, axis=1)
    position = (stride * jnp.arange(TOK_MB)[:, None] + jnp.arange(TOP)[None, :]) % chosen
    picked = shuffled[:, position]
    return picked.reshape(TOKENS, TOP).astype(jnp.int32)


def steps_of(key, extent, shards, least, largest):
    def one(dim, parts):
        draws = jax.random.uniform(jax.random.fold_in(jax.random.fold_in(key, 6), dim), (parts,), jnp.float32, least / len(shards), largest / len(shards))
        return jnp.repeat(jnp.exp(draws), extent[dim] // parts).reshape((-1,) + (1,) * (len(extent) - dim - 1))

    loudness = one(*shards[0])
    for cut in shards[1:]:
        loudness = loudness * one(*cut)
    return loudness


def normal_values(rng, shape, deviation, bound, split=(), kind=jnp.bfloat16):
    values = deviation * jax.random.normal(rng, shape, jnp.float32)
    if split:
        values = values * steps_of(rng, shape, split, -0.22, 0.18)
    return jnp.clip(values, -bound, bound).astype(kind)


def setup_inputs(seed: int = 0) -> dict:
    seeds = jax.random.split(jax.random.key(seed), 7)
    return {
        "tokens": normal_values(seeds[0], (TOKENS, D), 1.0, 6.0, ((0, 128), (1, 4))),
        "routes": draw_routes(jax.random.fold_in(seeds[6], 71), 0),
        "router_probs": jnp.clip(jnp.exp(math.log(1.0) - 3.912023 * jax.random.uniform(seeds[2], (TOKENS, TOP), jnp.float32) ** steps_of(seeds[2], (TOKENS, TOP), ((0, 128),), -0.2, 0.2)), 0.02, 1.0),
        "w_gate": normal_values(seeds[3], (EXPERTS, FF, D), D ** -0.5, 0.09375, ((0, 128), (1, 4))),
        "w_up": normal_values(seeds[4], (EXPERTS, FF, D), D ** -0.5, 0.09375, ((0, 128), (1, 4))),
        "w_down": normal_values(seeds[5], (EXPERTS, FF, D), (FF // 4) ** -0.5, 0.4375, ((0, 128), (1, 4))),
    }


def slot_ranks(flat_routes):
    same_expert = flat_routes[..., :, None] == flat_routes[..., None, :]
    count = flat_routes.shape[-1]
    earlier = jnp.arange(count)[:, None] > jnp.arange(count)[None, :]
    return jnp.sum(jnp.logical_and(same_expert, earlier), axis=-1).astype(jnp.int32)


def reference(tokens, routes, router_probs, w_gate, w_up, w_down):
    width = TOK_MB * TOP
    block_routes = routes.reshape(N_EXPERT, MICRO, width).astype(jnp.int32)
    slot_rank = slot_ranks(block_routes)
    mixing = router_probs / jnp.sum(router_probs, axis=-1, keepdims=True)
    mixing = mixing.reshape(N_EXPERT, MICRO, width)
    token_id = jnp.broadcast_to(jnp.arange(TOKENS, dtype=jnp.int32).reshape(N_EXPERT, MICRO, TOK_MB, 1), (N_EXPERT, MICRO, TOK_MB, TOP)).reshape(N_EXPERT, MICRO, width)
    source_id = jnp.broadcast_to(jnp.arange(N_EXPERT, dtype=jnp.int32)[:, None, None], block_routes.shape)
    micro_id = jnp.broadcast_to(jnp.arange(MICRO, dtype=jnp.int32)[None, :, None], block_routes.shape)
    table_tok = jnp.zeros((EXPERTS, MICRO, N_EXPERT, CAP), jnp.int32).at[block_routes, micro_id, source_id, slot_rank].set(token_id)
    table_mix = jnp.zeros((EXPERTS, MICRO, N_EXPERT, CAP), jnp.float32).at[block_routes, micro_id, source_id, slot_rank].set(mixing)
    share = FF // N_PAIR

    def one_expert(total, inputs):
        tok_ids, mix_w, gate_mat, up_mat, down_mat = inputs
        indices = tok_ids.reshape(-1)
        picked = tokens[indices]
        gate_act = jnp.dot(picked, gate_mat.T, preferred_element_type=jnp.float32)
        up_act = jnp.dot(picked, up_mat.T, preferred_element_type=jnp.float32)
        hidden = (jax.nn.silu(gate_act) * up_act).astype(jnp.bfloat16)
        outcome = jnp.zeros((indices.shape[0], D), jnp.float32)
        for piece in range(N_PAIR):
            term = jnp.dot(hidden[:, piece * share:(piece + 1) * share], down_mat[piece * share:(piece + 1) * share], preferred_element_type=jnp.float32)
            rounded = lax.optimization_barrier(term.astype(jnp.bfloat16))
            outcome = outcome + rounded.astype(jnp.float32)
        total = total.at[indices].add(mix_w.reshape(-1)[:, None] * outcome)
        return total, None

    total, _ = lax.scan(one_expert, jnp.zeros((TOKENS, D), jnp.float32), (table_tok, table_mix, w_gate, w_up, w_down))
    return total.astype(jnp.bfloat16)
```

```python
import jax
import jax.numpy as jnp
from jax import lax
from jax.experimental import pallas as pl
from jax.experimental.pallas import tpu as pltpu
from jax.sharding import PartitionSpec as P

TOK = 16
TOP = 8
RING = 8
EXPERTS = 128
SLOTS = 256
WIDTH = 1024
HID = 192
DV = (0, 1, 7, 2, 6, 3, 5, 4)
GROUPS = 2
PAIRS_G = RING // GROUPS
ROWS_G = SLOTS // GROUPS
HALF_G = ROWS_G // 2
LAG = 2
MSG = WIDTH + 2 * SLOTS
F32 = jnp.float32
BF16 = jnp.bfloat16


def dot_nt(a, b):
    return lax.dot_general(a, b, (((1,), (1,)), ((), ())), preferred_element_type=F32)


def dot_nn(a, b):
    return lax.dot_general(a, b, (((1,), (0,)), ((), ())), preferred_element_type=F32)


def spread_matrix(u, v, c, su, sv):
    slot = lax.broadcasted_iota(jnp.int32, (SLOTS, 2 * EXPERTS), 0)
    column = lax.broadcasted_iota(jnp.int32, (SLOTS, 2 * EXPERTS), 1)
    pair = slot >> 5
    odd = pair & 1
    dv = jnp.where(odd == 1, (pair + 1) >> 1, (8 - (pair >> 1)) & 7)
    dc = (slot >> 4) & 1
    rank = slot & 1
    owner = u * su + ((dv + v) & 7) * sv + ((dc + c) & 1)
    return jnp.where(column == rank * EXPERTS + owner, 1.0, 0.0).astype(BF16)


def kernel(
    tok, routes, probs, wg, wu, wd, out,
    wgv, wuv, wdv, stg, outb, xb, mix_hi, mix_lo, hid, a_out, a_in, b_late, b_out, b_in, y_out, back, z_out, z_in,
    w_sem, s1s, s1r, s2s, s2r, xss, xsr, fws, fwr, ras, rar, rbs, rbr, s3s, s3r, s4s, s4r,
):
    e = lax.axis_index("expert")
    x = lax.axis_index("pair")
    c = e % 2
    y = (e // 2) % RING
    z = e // (2 * RING)
    right = (x + 1) % 4
    left = (x + 3) % 4

    def role(core):
        u = (1 - core) * z + core * y
        v = (1 - core) * y + core * z
        return u, v, 16 - 14 * core, 2 + 14 * core

    u, v, su, sv = role(c)

    loads = []
    for k in range(4):
        quarter = pl.ds(pl.multiple_of(((x + 4 - k) % 4) * WIDTH, WIDTH), WIDTH)
        for j, (src, dst) in enumerate(((wg, wgv), (wu, wuv), (wd, wdv))):
            copy = pltpu.make_async_copy(src.at[0, :, quarter], dst.at[k], w_sem.at[3 * k + j])
            copy.start()
            loads.append(copy)

    barrier = pltpu.get_barrier_semaphore()

    def greet(expert, pair):
        pl.semaphore_signal(barrier, inc=1, device_id=(expert, pair), device_id_type=pl.DeviceIdType.MESH)

    for d in range(1, RING):
        for core in range(2):
            greet(((z + d) % RING) * 16 + y * 2 + core, x)
            greet(z * 16 + ((y + d) % RING) * 2 + core, x)
    greet(z * 16 + y * 2 + (1 - c), x)
    greet(e, right)
    greet(e, left)

    prob = probs[...]
    mixing = prob / jnp.sum(prob, axis=1, keepdims=True)
    chosen = routes[...]
    lanes = lax.broadcasted_iota(jnp.int32, (TOK, EXPERTS), 1)
    mix = jnp.zeros((TOK, EXPERTS), F32)
    for k in range(TOP):
        mix = jnp.where(chosen[:, k:k + 1] == lanes, mixing[:, k:k + 1], mix)
    named = jnp.where(mix > 0, 1.0, 0.0)
    row = lax.broadcasted_iota(jnp.int32, (TOK, TOK), 0)
    col = lax.broadcasted_iota(jnp.int32, (TOK, TOK), 1)
    earlier = dot_nn(jnp.where(row > col, 1.0, 0.0).astype(BF16), named.astype(BF16))
    second = earlier > 0.5
    for r in range(2):
        part = jnp.where(second, mix, 0.0) if r else jnp.where(second, 0.0, mix)
        high = part.astype(BF16)
        low = (part - high.astype(F32)).astype(BF16)
        stg[0:TOK, WIDTH + r * EXPERTS:WIDTH + (r + 1) * EXPERTS] = high
        stg[0:TOK, WIDTH + SLOTS + r * EXPERTS:WIDTH + SLOTS + (r + 1) * EXPERTS] = low
    stg[0:TOK, 0:WIDTH] = tok[...]

    pl.semaphore_wait(barrier, 31)

    def remote(src, dst, send, recv, expert, pair):
        return pltpu.make_async_remote_copy(
            src_ref=src, dst_ref=dst, send_sem=send, recv_sem=recv,
            device_id=(expert, pair), device_id_type=pl.DeviceIdType.MESH,
        )

    gathers = []
    for du in (1, 7, 2, 6, 3, 5, 4):
        copy = remote(
            stg.at[0:TOK, :], stg.at[du * TOK:(du + 1) * TOK, :], s1s.at[du - 1], s1r.at[du - 1],
            ((u + du) % RING) * su + v * sv + c, x,
        )
        copy.start()
        gathers.append(copy)
    spread = spread_matrix(u, v, c, su, sv)
    for copy in gathers:
        copy.wait_recv()

    source = stg[:, WIDTH:WIDTH + SLOTS]
    tok_du = lax.broadcasted_iota(jnp.int32, (SLOTS, RING * TOK), 1) >> 4
    slot_du = (lax.broadcasted_iota(jnp.int32, (SLOTS, RING * TOK), 0) >> 1) & 7
    placing = jnp.where(jnp.logical_and(dot_nt(spread, source) > 0, tok_du == slot_du), 1.0, 0.0).astype(BF16)
    routed = [None] * 16
    for g in range(GROUPS):
        rows = dot_nn(placing[g * ROWS_G:(g + 1) * ROWS_G, :], stg[:, 0:WIDTH]).astype(BF16)
        outb[g * ROWS_G:(g + 1) * ROWS_G, :] = rows
        if g == 0:
            xb[0, 0:TOK, :] = rows[0:TOK, :]
        for i in range(g * PAIRS_G, (g + 1) * PAIRS_G):
            for dc in range(2):
                j = 2 * i + dc
                if j == 0:
                    continue
                copy = remote(
                    outb.at[j * 16:(j + 1) * 16, :], xb.at[0, j * 16:(j + 1) * 16, :], s2s.at[j], s2r.at[j],
                    u * su + ((v + DV[i]) % RING) * sv + (c + dc) % 2, x,
                )
                copy.start()
                routed[j] = copy

    tok_du = lax.broadcasted_iota(jnp.int32, (RING * TOK, SLOTS), 0) >> 4
    slot_du = (lax.broadcasted_iota(jnp.int32, (RING * TOK, SLOTS), 1) >> 1) & 7
    same = tok_du == slot_du
    mix_hi[...] = jnp.where(same, dot_nt(source, spread), 0.0).astype(BF16)
    mix_lo[...] = jnp.where(same, dot_nt(stg[:, WIDTH + SLOTS:MSG], spread), 0.0).astype(BF16)

    sent = [[None] * RING, [None] * RING]
    forwarded = [[None] * RING, [None] * RING]

    def send_pair(i):
        rows = slice(32 * i, 32 * i + 32)
        for dc in range(2):
            if 2 * i + dc:
                routed[2 * i + dc].wait_recv()
        for way, (k, target) in enumerate(((1, right), (3, left))):
            copy = remote(xb.at[0, rows, :], xb.at[k, rows, :], xss.at[way, i], xsr.at[way, i], e, target)
            copy.start()
            sent[way][i] = copy

    def forward_pair(i):
        for way, (k, target) in enumerate(((1, right), (3, left))):
            rows = slice(32 * i + 16 * way, 32 * i + 16 * way + 16)
            sent[way][i].wait_recv()
            copy = remote(xb.at[k, rows, :], xb.at[2, rows, :], fws.at[way, i], fwr.at[way, i], e, target)
            copy.start()
            forwarded[way][i] = copy

    def hidden(g):
        rows = slice(g * ROWS_G, (g + 1) * ROWS_G)
        for i in range(g * PAIRS_G, (g + 1) * PAIRS_G):
            for way in range(2):
                forwarded[way][i].wait_recv()
        gate = jnp.zeros((ROWS_G, HID), F32)
        up = jnp.zeros((ROWS_G, HID), F32)
        for k in range(4):
            gate = gate + dot_nt(xb[k, rows, :], wgv[k])
            up = up + dot_nt(xb[k, rows, :], wuv[k])
        hid[rows, :] = (gate / (1.0 + jnp.exp(-gate)) * up).astype(BF16)

    far = [None] * GROUPS
    near = [None] * GROUPS

    def down(g, k):
        return dot_nn(hid[g * ROWS_G:(g + 1) * ROWS_G, :], wdv[k])

    def halves(way):
        return slice(way * HALF_G, (way + 1) * HALF_G), slice((1 - way) * HALF_G, (2 - way) * HALF_G)

    def send_far(g):
        a_out[g] = down(g, 2).astype(BF16)
        far[g] = []
        for way, target in enumerate((right, left)):
            copy = remote(a_out.at[g, halves(way)[0], :], a_in.at[way, g], ras.at[way, g], rar.at[way, g], e, target)
            copy.start()
            far[g].append(copy)

    def send_near(way, g, rows, late):
        target = left if way else right
        copy = remote(
            b_out.at[way, g, rows, :], b_in.at[way, g, rows, :],
            rbs.at[way, g, late], rbr.at[way, g, late], e, target,
        )
        copy.start()
        near[g].append(copy)

    def send_near_free(g):
        near[g] = []
        for way, k in enumerate((3, 1)):
            late, free = halves(way)
            term = down(g, k)
            b_late[way, g] = term[late, :]
            b_out[way, g, free, :] = term[free, :].astype(BF16)
            send_near(way, g, free, 0)

    def send_near_late(g):
        for way in range(2):
            late, _ = halves(way)
            far[g][way].wait_recv()
            b_out[way, g, late, :] = (b_late[way, g] + a_in[way, g].astype(F32)).astype(BF16)
            send_near(way, g, late, 1)

    returned = [None] * 16

    def send_back(g):
        rows = slice(g * ROWS_G, (g + 1) * ROWS_G)
        term = down(g, 0)
        for copy in near[g]:
            copy.wait_recv()
        total = (term + b_in[0, g].astype(F32) + b_in[1, g].astype(F32)).astype(BF16)
        y_out[rows, :] = total
        if g == 0:
            back[0:TOK, :] = total[0:TOK, :]
        for i in range(g * PAIRS_G, (g + 1) * PAIRS_G):
            for dc in range(2):
                j = 2 * i + dc
                if j == 0:
                    continue
                core = (c + dc) % 2
                u_s, v_s, su_s, sv_s = role(core)
                copy = remote(
                    y_out.at[j * 16:(j + 1) * 16, :], back.at[j * 16:(j + 1) * 16, :], s3s.at[j], s3r.at[j],
                    u_s * su_s + ((v_s + RING - DV[i]) % RING) * sv_s + core, x,
                )
                copy.start()
                returned[j] = copy

    for i in range(RING):
        send_pair(i)
        if i >= LAG:
            forward_pair(i - LAG)
    for copy in loads:
        copy.wait()
    hidden(0)
    for i in range(RING - LAG, RING):
        forward_pair(i)
    send_far(0)
    send_near_free(0)
    for g in range(1, GROUPS):
        hidden(g)
        send_far(g)
        send_near_late(g - 1)
        send_near_free(g)
        send_back(g - 1)
    send_near_late(GROUPS - 1)
    send_back(GROUPS - 1)

    mixture = jnp.zeros((RING * TOK, WIDTH), F32)
    for g in range(GROUPS):
        rows = slice(g * ROWS_G, (g + 1) * ROWS_G)
        for j in range(g * 2 * PAIRS_G, (g + 1) * 2 * PAIRS_G):
            if j:
                returned[j].wait_recv()
        mixture = mixture + dot_nn(mix_hi[:, rows], back[rows, :]) + dot_nn(mix_lo[:, rows], back[rows, :])
    z_out[...] = mixture.astype(BF16)
    homes = []
    for du in (1, 7, 2, 6, 3, 5, 4):
        copy = remote(
            z_out.at[du * TOK:(du + 1) * TOK, :], z_in.at[du], s4s.at[du - 1], s4r.at[du - 1],
            ((u + RING - du) % RING) * su + v * sv + c, x,
        )
        copy.start()
        homes.append(copy)
    total = mixture[0:TOK, :]
    for du, copy in zip((1, 7, 2, 6, 3, 5, 4), homes):
        copy.wait_recv()
        total = total + z_in[du].astype(F32)
    out[...] = total.astype(BF16)

    for copy in gathers + routed[1:] + sum(sent + forwarded + far + near, []) + returned[1:] + homes:
        copy.wait_send()


def per_device(tokens, routes, router_probs, w_gate, w_up, w_down):
    vmem = pl.BlockSpec(memory_space=pltpu.VMEM)
    hbm = pl.BlockSpec(memory_space=pl.ANY)
    dma = pltpu.SemaphoreType.DMA
    return pl.pallas_call(
        kernel,
        out_shape=jax.ShapeDtypeStruct((TOK, WIDTH), BF16),
        in_specs=[vmem] * 3 + [hbm] * 3,
        out_specs=vmem,
        scratch_shapes=[
            pltpu.VMEM((4, HID, WIDTH), BF16),
            pltpu.VMEM((4, HID, WIDTH), BF16),
            pltpu.VMEM((4, HID, WIDTH), BF16),
            pltpu.VMEM((RING * TOK, MSG), BF16),
            pltpu.VMEM((SLOTS, WIDTH), BF16),
            pltpu.VMEM((4, SLOTS, WIDTH), BF16),
            pltpu.VMEM((RING * TOK, SLOTS), BF16),
            pltpu.VMEM((RING * TOK, SLOTS), BF16),
            pltpu.VMEM((SLOTS, HID), BF16),
            pltpu.VMEM((GROUPS, ROWS_G, WIDTH), BF16),
            pltpu.VMEM((2, GROUPS, HALF_G, WIDTH), BF16),
            pltpu.VMEM((2, GROUPS, HALF_G, WIDTH), F32),
            pltpu.VMEM((2, GROUPS, ROWS_G, WIDTH), BF16),
            pltpu.VMEM((2, GROUPS, ROWS_G, WIDTH), BF16),
            pltpu.VMEM((SLOTS, WIDTH), BF16),
            pltpu.VMEM((SLOTS, WIDTH), BF16),
            pltpu.VMEM((RING * TOK, WIDTH), BF16),
            pltpu.VMEM((RING, TOK, WIDTH), BF16),
            dma((12,)),
            dma((7,)), dma((7,)),
            dma((16,)), dma((16,)),
            dma((2, RING)), dma((2, RING)),
            dma((2, RING)), dma((2, RING)),
            dma((2, GROUPS)), dma((2, GROUPS)),
            dma((2, GROUPS, 2)), dma((2, GROUPS, 2)),
            dma((16,)), dma((16,)),
            dma((7,)), dma((7,)),
        ],
        compiler_params=pltpu.CompilerParams(
            collective_id=0, has_side_effects=True, vmem_limit_bytes=48 * 1024 * 1024
        ),
    )(tokens, routes, router_probs, w_gate, w_up, w_down)


def solution(mesh):
    in_specs = (
        P("expert", "pair"),
        P("expert", None),
        P("expert", None),
        P("expert", "pair", None),
        P("expert", "pair", None),
        P("expert", "pair", None),
    )
    out_specs = P("expert", "pair")
    return jax.shard_map(
        per_device, mesh=mesh, in_specs=in_specs, out_specs=out_specs, check_vma=False
    )
```

```python
import jax
import jax.numpy as jnp
from jax import lax
from jax.experimental import pallas as pl
from jax.experimental.pallas import tpu as pltpu
from jax.sharding import PartitionSpec as P

TOK = 16
TOP = 8
RING = 8
EXPERTS = 128
SLOTS = 256
WIDTH = 1024
HID = 192
DV = (0, 1, 7, 2, 6, 3, 5, 4)
GROUPS = 2
PAIRS_G = RING // GROUPS
ROWS_G = SLOTS // GROUPS
HALF_G = ROWS_G // 2
LAG = 2
MSG = WIDTH + 128
FAR_FIRST = (4, 3, 5, 2, 6, 1, 7)
F32 = jnp.float32
BF16 = jnp.bfloat16


def dot_nt(a, b):
    return lax.dot_general(a, b, (((1,), (1,)), ((), ())), preferred_element_type=F32)


def dot_nn(a, b):
    return lax.dot_general(a, b, (((1,), (0,)), ((), ())), preferred_element_type=F32)


def iota(shape, dim):
    return lax.broadcasted_iota(jnp.int32, shape, dim)


def ones_where(condition):
    return jnp.where(condition, 1.0, 0.0).astype(BF16)


def kernel(
    tok_hbm, routes_hbm, probs_hbm, wg, wu, wd, out,
    routes, probs, wgv, wuv, wdv, pieces, snd, stg, outb, xb, mix_hi, mix_lo, hid, a_out, a_in, b_late, b_out, b_in, y_out, back, z_out, z_in,
    in_sem, w_sem, s1s, s1r, s2s, s2r, xss, xsr, fws, fwr, ras, rar, rbs, rbr, s3s, s3r, s4s, s4r,
):
    e = lax.axis_index("expert")
    x = lax.axis_index("pair")
    c = e % 2
    y = (e // 2) % RING
    z = e // (2 * RING)
    right = (x + 1) % 4
    left = (x + 3) % 4

    def role(core):
        u = (1 - core) * z + core * y
        v = (1 - core) * y + core * z
        return u, v, 16 - 14 * core, 2 + 14 * core

    u, v, su, sv = role(c)

    barrier = pltpu.get_barrier_semaphore()

    def greet(expert, pair):
        pl.semaphore_signal(barrier, inc=1, device_id=(expert, pair), device_id_type=pl.DeviceIdType.MESH)

    for d in FAR_FIRST:
        for core in range(2):
            greet(((z + d) % RING) * 16 + y * 2 + core, x)
            greet(z * 16 + ((y + d) % RING) * 2 + core, x)
    greet(z * 16 + y * 2 + (1 - c), x)
    greet(e, right)
    greet(e, left)

    inputs = [
        pltpu.make_async_copy(routes_hbm, routes, in_sem.at[8]),
        pltpu.make_async_copy(probs_hbm, probs, in_sem.at[9]),
        pltpu.make_async_copy(tok_hbm, stg.at[0:TOK, 0:WIDTH], in_sem.at[0]),
    ]
    for du in FAR_FIRST:
        inputs.append(pltpu.make_async_copy(tok_hbm, snd.at[du, :, 0:WIDTH], in_sem.at[du]))
    for copy in inputs:
        copy.start()

    loads = []
    for k in range(4):
        quarter = pl.ds(pl.multiple_of(((x + 4 - k) % 4) * WIDTH, WIDTH), WIDTH)
        for j, (src, dst) in enumerate(((wg, wgv), (wu, wuv), (wd, wdv))):
            copy = pltpu.make_async_copy(src.at[0, :, quarter], dst.at[k], w_sem.at[3 * k + j])
            copy.start()
            loads.append(copy)

    inputs[0].wait()
    inputs[1].wait()
    prob = probs[...]
    mixing = prob / jnp.sum(prob, axis=0, keepdims=True)
    chosen = routes[...]
    experts = iota((EXPERTS, TOK), 0)
    mix = jnp.zeros((EXPERTS, TOK), F32)
    for k in range(TOP):
        mix = jnp.where(chosen[k:k + 1, :] == experts, mixing[k:k + 1, :], mix)
    named = jnp.where(mix > 0, 1.0, 0.0).astype(BF16)
    row, col = iota((TOK, TOK), 0), iota((TOK, TOK), 1)
    second = dot_nn(named, ones_where(row < col)) > 0.5
    same_token = ones_where(row == col)
    for r in range(2):
        part = jnp.where(second, mix, 0.0) if r else jnp.where(second, 0.0, mix)
        high = part.astype(BF16)
        low = (part - high.astype(F32)).astype(BF16)
        for j, piece in enumerate((high, low)):
            start = (2 * j + r) * EXPERTS
            pieces[:, start:start + EXPERTS] = dot_nt(same_token, piece).astype(BF16)
    lane = iota((RING * 128, 1), 0)
    pair = (lane >> 2) & 7
    offset = jnp.where((pair & 1) == 1, (pair + 1) >> 1, (8 - (pair >> 1)) & 7)
    owner = ((u + (lane >> 7)) & 7) * su + ((v + offset) & 7) * sv + ((c + (lane >> 1)) & 1)
    column = ((lane >> 5) & 3) * 2 * EXPERTS + (lane & 1) * EXPERTS + owner
    pick = ones_where(iota((RING * 128, 4 * EXPERTS), 1) == column)
    blocks = dot_nt(pieces[...], pick).astype(BF16)
    stg[0:TOK, WIDTH:MSG] = blocks[:, 0:128]
    for du in range(1, RING):
        snd[du, :, WIDTH:MSG] = blocks[:, du * 128:(du + 1) * 128]
    for copy in inputs[2:]:
        copy.wait()

    pl.semaphore_wait(barrier, 31)

    def remote(src, dst, send, recv, expert, pair):
        return pltpu.make_async_remote_copy(
            src_ref=src, dst_ref=dst, send_sem=send, recv_sem=recv,
            device_id=(expert, pair), device_id_type=pl.DeviceIdType.MESH,
        )

    gathers = []
    for du in FAR_FIRST:
        copy = remote(
            snd.at[du], stg.at[du * TOK:(du + 1) * TOK, :], s1s.at[du - 1], s1r.at[du - 1],
            ((u + du) % RING) * su + v * sv + c, x,
        )
        copy.start()
        gathers.append(copy)
    slot = iota((SLOTS, 128), 0)
    spread = [ones_where(iota((SLOTS, 128), 1) == 32 * j + ((slot >> 4) << 1) + (slot & 1)) for j in range(2)]
    for copy in gathers:
        copy.wait_recv()

    source = stg[:, WIDTH:MSG]
    tok_du = iota((SLOTS, RING * TOK), 1) >> 4
    slot_du = (iota((SLOTS, RING * TOK), 0) >> 1) & 7
    placing = ones_where(jnp.logical_and(dot_nt(spread[0], source) > 0, tok_du == slot_du))
    routed = [None] * 16
    for g in range(GROUPS):
        rows = dot_nn(placing[g * ROWS_G:(g + 1) * ROWS_G, :], stg[:, 0:WIDTH]).astype(BF16)
        outb[g * ROWS_G:(g + 1) * ROWS_G, :] = rows
        if g == 0:
            xb[0, 0:TOK, :] = rows[0:TOK, :]
        for i in range(g * PAIRS_G, (g + 1) * PAIRS_G):
            for dc in range(2):
                j = 2 * i + dc
                if j == 0:
                    continue
                copy = remote(
                    outb.at[j * 16:(j + 1) * 16, :], xb.at[0, j * 16:(j + 1) * 16, :], s2s.at[j], s2r.at[j],
                    u * su + ((v + DV[i]) % RING) * sv + (c + dc) % 2, x,
                )
                copy.start()
                routed[j] = copy

    tok_du = iota((RING * TOK, SLOTS), 0) >> 4
    slot_du = (iota((RING * TOK, SLOTS), 1) >> 1) & 7
    same = tok_du == slot_du
    mix_hi[...] = jnp.where(same, dot_nt(source, spread[0]), 0.0).astype(BF16)
    mix_lo[...] = jnp.where(same, dot_nt(source, spread[1]), 0.0).astype(BF16)

    sent = [[None] * RING, [None] * RING]
    forwarded = [[None] * RING, [None] * RING]

    def send_pair(i):
        rows = slice(32 * i, 32 * i + 32)
        for dc in range(2):
            if 2 * i + dc:
                routed[2 * i + dc].wait_recv()
        for way, (k, target) in enumerate(((1, right), (3, left))):
            copy = remote(xb.at[0, rows, :], xb.at[k, rows, :], xss.at[way, i], xsr.at[way, i], e, target)
            copy.start()
            sent[way][i] = copy

    def forward_pair(i):
        for way, (k, target) in enumerate(((1, right), (3, left))):
            rows = slice(32 * i + 16 * way, 32 * i + 16 * way + 16)
            sent[way][i].wait_recv()
            copy = remote(xb.at[k, rows, :], xb.at[2, rows, :], fws.at[way, i], fwr.at[way, i], e, target)
            copy.start()
            forwarded[way][i] = copy

    def hidden(g):
        rows = slice(g * ROWS_G, (g + 1) * ROWS_G)
        for i in range(g * PAIRS_G, (g + 1) * PAIRS_G):
            for way in range(2):
                forwarded[way][i].wait_recv()
        gate = jnp.zeros((ROWS_G, HID), F32)
        up = jnp.zeros((ROWS_G, HID), F32)
        for k in range(4):
            gate = gate + dot_nt(xb[k, rows, :], wgv[k])
            up = up + dot_nt(xb[k, rows, :], wuv[k])
        hid[rows, :] = (gate / (1.0 + jnp.exp(-gate)) * up).astype(BF16)

    far = [None] * GROUPS
    near = [None] * GROUPS

    def down(g, k):
        return dot_nn(hid[g * ROWS_G:(g + 1) * ROWS_G, :], wdv[k])

    def halves(way):
        return slice(way * HALF_G, (way + 1) * HALF_G), slice((1 - way) * HALF_G, (2 - way) * HALF_G)

    def send_far(g):
        a_out[g] = down(g, 2).astype(BF16)
        far[g] = []
        for way, target in enumerate((right, left)):
            copy = remote(a_out.at[g, halves(way)[0], :], a_in.at[way, g], ras.at[way, g], rar.at[way, g], e, target)
            copy.start()
            far[g].append(copy)

    def send_near(way, g, rows, late):
        target = left if way else right
        copy = remote(
            b_out.at[way, g, rows, :], b_in.at[way, g, rows, :],
            rbs.at[way, g, late], rbr.at[way, g, late], e, target,
        )
        copy.start()
        near[g].append(copy)

    def send_near_free(g):
        near[g] = []
        for way, k in enumerate((3, 1)):
            late, free = halves(way)
            term = down(g, k)
            b_late[way, g] = term[late, :]
            b_out[way, g, free, :] = term[free, :].astype(BF16)
            send_near(way, g, free, 0)

    def send_near_late(g):
        for way in range(2):
            late, _ = halves(way)
            far[g][way].wait_recv()
            b_out[way, g, late, :] = (b_late[way, g] + a_in[way, g].astype(F32)).astype(BF16)
            send_near(way, g, late, 1)

    returned = [None] * 16

    def send_back(g):
        rows = slice(g * ROWS_G, (g + 1) * ROWS_G)
        term = down(g, 0)
        for copy in near[g]:
            copy.wait_recv()
        total = (term + b_in[0, g].astype(F32) + b_in[1, g].astype(F32)).astype(BF16)
        y_out[rows, :] = total
        if g == 0:
            back[0:TOK, :] = total[0:TOK, :]
        for i in range(g * PAIRS_G, (g + 1) * PAIRS_G):
            for dc in range(2):
                j = 2 * i + dc
                if j == 0:
                    continue
                core = (c + dc) % 2
                u_s, v_s, su_s, sv_s = role(core)
                copy = remote(
                    y_out.at[j * 16:(j + 1) * 16, :], back.at[j * 16:(j + 1) * 16, :], s3s.at[j], s3r.at[j],
                    u_s * su_s + ((v_s + RING - DV[i]) % RING) * sv_s + core, x,
                )
                copy.start()
                returned[j] = copy

    for i in range(RING):
        send_pair(i)
        if i >= LAG:
            forward_pair(i - LAG)
    for copy in loads:
        copy.wait()
    hidden(0)
    for i in range(RING - LAG, RING):
        forward_pair(i)
    send_far(0)
    send_near_free(0)
    for g in range(1, GROUPS):
        hidden(g)
        send_far(g)
        send_near_late(g - 1)
        send_near_free(g)
        send_back(g - 1)
    send_near_late(GROUPS - 1)
    send_back(GROUPS - 1)

    mixture = jnp.zeros((RING * TOK, WIDTH), F32)
    for g in range(GROUPS):
        rows = slice(g * ROWS_G, (g + 1) * ROWS_G)
        for j in range(g * 2 * PAIRS_G, (g + 1) * 2 * PAIRS_G):
            if j:
                returned[j].wait_recv()
        mixture = mixture + dot_nn(mix_hi[:, rows], back[rows, :]) + dot_nn(mix_lo[:, rows], back[rows, :])
    z_out[...] = mixture.astype(BF16)
    homes = []
    for du in FAR_FIRST:
        copy = remote(
            z_out.at[du * TOK:(du + 1) * TOK, :], z_in.at[du], s4s.at[du - 1], s4r.at[du - 1],
            ((u + RING - du) % RING) * su + v * sv + c, x,
        )
        copy.start()
        homes.append(copy)
    total = mixture[0:TOK, :]
    for du, copy in zip(FAR_FIRST, homes):
        copy.wait_recv()
        total = total + z_in[du].astype(F32)
    out[...] = total.astype(BF16)

    for copy in gathers + routed[1:] + sum(sent + forwarded + far + near, []) + returned[1:] + homes:
        copy.wait_send()


def per_device(tokens, routes, router_probs, w_gate, w_up, w_down):
    vmem = pl.BlockSpec(memory_space=pltpu.VMEM)
    hbm = pl.BlockSpec(memory_space=pltpu.HBM)
    dma = pltpu.SemaphoreType.DMA
    return pl.pallas_call(
        kernel,
        out_shape=jax.ShapeDtypeStruct((TOK, WIDTH), BF16),
        in_specs=[hbm] * 6,
        out_specs=vmem,
        scratch_shapes=[
            pltpu.VMEM((TOP, TOK), jnp.int32),
            pltpu.VMEM((TOP, TOK), F32),
            pltpu.VMEM((4, HID, WIDTH), BF16),
            pltpu.VMEM((4, HID, WIDTH), BF16),
            pltpu.VMEM((4, HID, WIDTH), BF16),
            pltpu.VMEM((TOK, 4 * EXPERTS), BF16),
            pltpu.VMEM((RING, TOK, MSG), BF16),
            pltpu.VMEM((RING * TOK, MSG), BF16),
            pltpu.VMEM((SLOTS, WIDTH), BF16),
            pltpu.VMEM((4, SLOTS, WIDTH), BF16),
            pltpu.VMEM((RING * TOK, SLOTS), BF16),
            pltpu.VMEM((RING * TOK, SLOTS), BF16),
            pltpu.VMEM((SLOTS, HID), BF16),
            pltpu.VMEM((GROUPS, ROWS_G, WIDTH), BF16),
            pltpu.VMEM((2, GROUPS, HALF_G, WIDTH), BF16),
            pltpu.VMEM((2, GROUPS, HALF_G, WIDTH), F32),
            pltpu.VMEM((2, GROUPS, ROWS_G, WIDTH), BF16),
            pltpu.VMEM((2, GROUPS, ROWS_G, WIDTH), BF16),
            pltpu.VMEM((SLOTS, WIDTH), BF16),
            pltpu.VMEM((SLOTS, WIDTH), BF16),
            pltpu.VMEM((RING * TOK, WIDTH), BF16),
            pltpu.VMEM((RING, TOK, WIDTH), BF16),
            dma((10,)),
            dma((12,)),
            dma((7,)), dma((7,)),
            dma((16,)), dma((16,)),
            dma((2, RING)), dma((2, RING)),
            dma((2, RING)), dma((2, RING)),
            dma((2, GROUPS)), dma((2, GROUPS)),
            dma((2, GROUPS, 2)), dma((2, GROUPS, 2)),
            dma((16,)), dma((16,)),
            dma((7,)), dma((7,)),
        ],
        compiler_params=pltpu.CompilerParams(
            collective_id=0, has_side_effects=True, vmem_limit_bytes=62 * 1024 * 1024
        ),
    )(tokens, routes.T, router_probs.T, w_gate, w_up, w_down)


def solution(mesh):
    in_specs = (
        P("expert", "pair"),
        P("expert", None),
        P("expert", None),
        P("expert", "pair", None),
        P("expert", "pair", None),
        P("expert", "pair", None),
    )
    out_specs = P("expert", "pair")
    return jax.shard_map(
        per_device, mesh=mesh, in_specs=in_specs, out_specs=out_specs, check_vma=False
    )
```

```python
import jax
import jax.numpy as jnp
from jax import lax
from jax.experimental import pallas as pl
from jax.experimental.pallas import tpu as pltpu
from jax.sharding import PartitionSpec as P

TOK = 16
TOP = 8
RING = 8
EXPERTS = 128
SLOTS = 256
WIDTH = 1024
HID = 192
DV = (0, 1, 7, 2, 6, 3, 5, 4)
GROUPS = 2
PAIRS_G = RING // GROUPS
ROWS_G = SLOTS // GROUPS
HALF_G = ROWS_G // 2
LAG = 2
EARLY_AFTER = 3
MSG = WIDTH + 128
EARLY = 384
LATE = WIDTH - EARLY
FAR_FIRST = (4, 3, 5, 2, 6, 1, 7)
F32 = jnp.float32
BF16 = jnp.bfloat16


def dot_nt(a, b):
    return lax.dot_general(a, b, (((1,), (1,)), ((), ())), preferred_element_type=F32)


def dot_nn(a, b):
    return lax.dot_general(a, b, (((1,), (0,)), ((), ())), preferred_element_type=F32)


def iota(shape, dim):
    return lax.broadcasted_iota(jnp.int32, shape, dim)


def ones_where(condition):
    return jnp.where(condition, 1.0, 0.0).astype(BF16)


def kernel(
    tok_hbm, routes_hbm, probs_hbm, wg, wu, wd, out,
    routes, probs, wgv, wuv, wdv, pieces, snd, stg, outb, own, ring, mix_hi, mix_lo, hid,
    a_out, a_in, b_late, b_out, b_in, y_out, back, z_out, z_in, early_tok, early_out, early, early_y, early_back, early_z, early_sum,
    in_sem, w_sem, s1s, s1r, s2s, s2r, xss, xsr, fws, fwr, ras, rar, rbs, rbr, s3s, s3r, s4s, s4r,
    ets, etr, ers, err, eys, eyr, ezs, ezr,
):
    e = lax.axis_index("expert")
    x = lax.axis_index("pair")
    c = e % 2
    y = (e // 2) % RING
    z = e // (2 * RING)
    right = (x + 1) % 4
    left = (x + 3) % 4

    def role(core):
        u = (1 - core) * z + core * y
        v = (1 - core) * y + core * z
        return u, v, 16 - 14 * core, 2 + 14 * core

    u, v, su, sv = role(c)

    barrier = pltpu.get_barrier_semaphore()

    def greet(expert, pair):
        pl.semaphore_signal(barrier, inc=1, device_id=(expert, pair), device_id_type=pl.DeviceIdType.MESH)

    for d in FAR_FIRST:
        for core in range(2):
            greet(((z + d) % RING) * 16 + y * 2 + core, x)
            greet(z * 16 + ((y + d) % RING) * 2 + core, x)
    greet(z * 16 + y * 2 + (1 - c), x)
    for k in range(1, 4):
        greet(e, (x + k) % 4)

    inputs = [
        pltpu.make_async_copy(routes_hbm, routes, in_sem.at[8]),
        pltpu.make_async_copy(probs_hbm, probs, in_sem.at[9]),
        pltpu.make_async_copy(tok_hbm, stg.at[0:TOK, 0:WIDTH], in_sem.at[0]),
    ]
    for du in FAR_FIRST:
        inputs.append(pltpu.make_async_copy(tok_hbm, snd.at[du, :, 0:WIDTH], in_sem.at[du]))
    for copy in inputs:
        copy.start()

    loads = []
    for k in range(4):
        quarter = pl.ds(pl.multiple_of(((x + 4 - k) % 4) * WIDTH, WIDTH), WIDTH)
        for j, (src, dst) in enumerate(((wg, wgv), (wu, wuv), (wd, wdv))):
            copy = pltpu.make_async_copy(src.at[0, :, quarter], dst.at[k], w_sem.at[3 * k + j])
            copy.start()
            loads.append(copy)

    inputs[0].wait()
    inputs[1].wait()
    prob = probs[...]
    mixing = prob / jnp.sum(prob, axis=0, keepdims=True)
    chosen = routes[...]
    experts = iota((EXPERTS, TOK), 0)
    mix = jnp.zeros((EXPERTS, TOK), F32)
    for k in range(TOP):
        mix = jnp.where(chosen[k:k + 1, :] == experts, mixing[k:k + 1, :], mix)
    named = jnp.where(mix > 0, 1.0, 0.0).astype(BF16)
    row, col = iota((TOK, TOK), 0), iota((TOK, TOK), 1)
    second = dot_nn(named, ones_where(row < col)) > 0.5
    same_token = ones_where(row == col)
    for r in range(2):
        part = jnp.where(second, mix, 0.0) if r else jnp.where(second, 0.0, mix)
        high = part.astype(BF16)
        low = (part - high.astype(F32)).astype(BF16)
        for j, piece in enumerate((high, low)):
            start = (2 * j + r) * EXPERTS
            pieces[:, start:start + EXPERTS] = dot_nt(same_token, piece).astype(BF16)
    lane = iota((RING * 128, 1), 0)
    pair = (lane >> 2) & 7
    offset = jnp.where((pair & 1) == 1, (pair + 1) >> 1, (8 - (pair >> 1)) & 7)
    owner = ((u + (lane >> 7)) & 7) * su + ((v + offset) & 7) * sv + ((c + (lane >> 1)) & 1)
    column = ((lane >> 5) & 3) * 2 * EXPERTS + (lane & 1) * EXPERTS + owner
    pick = ones_where(iota((RING * 128, 4 * EXPERTS), 1) == column)
    blocks = dot_nt(pieces[...], pick).astype(BF16)
    stg[0:TOK, WIDTH:MSG] = blocks[:, 0:128]
    for du in range(1, RING):
        snd[du, :, WIDTH:MSG] = blocks[:, du * 128:(du + 1) * 128]
    for copy in inputs[2:]:
        copy.wait()

    pl.semaphore_wait(barrier, 32)

    def remote(src, dst, send, recv, expert, pair):
        return pltpu.make_async_remote_copy(
            src_ref=src, dst_ref=dst, send_sem=send, recv_sem=recv,
            device_id=(expert, pair), device_id_type=pl.DeviceIdType.MESH,
        )

    gathers = []
    for du in FAR_FIRST:
        copy = remote(
            snd.at[du], stg.at[du * TOK:(du + 1) * TOK, :], s1s.at[du - 1], s1r.at[du - 1],
            ((u + du) % RING) * su + v * sv + c, x,
        )
        copy.start()
        gathers.append(copy)
    slot = iota((SLOTS, 128), 0)
    spread = [ones_where(iota((SLOTS, 128), 1) == 32 * j + ((slot >> 4) << 1) + (slot & 1)) for j in range(2)]
    for copy in gathers:
        copy.wait_recv()

    crossing = [None] * 3
    for k in (2, 1, 3):
        copy = remote(
            stg.at[:, LATE:WIDTH], early_tok.at[:, (k - 1) * EARLY:k * EARLY], ets.at[k - 1], etr.at[k - 1], e, (x + k) % 4
        )
        copy.start()
        crossing[k - 1] = copy

    source = stg[:, WIDTH:MSG]
    tok_du = iota((SLOTS, RING * TOK), 1) >> 4
    slot_du = (iota((SLOTS, RING * TOK), 0) >> 1) & 7
    placing = ones_where(jnp.logical_and(dot_nt(spread[0], source) > 0, tok_du == slot_du))
    routed = [None] * 16
    routed_early = [None] * 16

    def owner_of(j):
        return u * su + ((v + DV[j // 2]) % RING) * sv + (c + j % 2) % 2

    def rows_of(j):
        return slice(j * 16, (j + 1) * 16)

    def route_early():
        for copy in crossing:
            copy.wait_recv()
        early_out[...] = dot_nn(placing, early_tok[...]).astype(BF16)
        early[0:TOK, :] = early_out[0:TOK, :]
        for j in range(1, 16):
            copy = remote(early_out.at[rows_of(j), :], early.at[rows_of(j), :], ers.at[j], err.at[j], owner_of(j), x)
            copy.start()
            routed_early[j] = copy

    for g in range(GROUPS):
        rows = dot_nn(placing[g * ROWS_G:(g + 1) * ROWS_G, :], stg[:, 0:WIDTH]).astype(BF16)
        outb[g * ROWS_G:(g + 1) * ROWS_G, :] = rows
        if g == 0:
            own[0:TOK, :] = rows[0:TOK, :]
        for j in range(max(1, g * 2 * PAIRS_G), (g + 1) * 2 * PAIRS_G):
            copy = remote(outb.at[rows_of(j), :], own.at[rows_of(j), :], s2s.at[j], s2r.at[j], owner_of(j), x)
            copy.start()
            routed[j] = copy

    tok_du = iota((RING * TOK, SLOTS), 0) >> 4
    slot_du = (iota((RING * TOK, SLOTS), 1) >> 1) & 7
    same = tok_du == slot_du
    mix_hi[...] = jnp.where(same, dot_nt(source, spread[0]), 0.0).astype(BF16)
    mix_lo[...] = jnp.where(same, dot_nt(source, spread[1]), 0.0).astype(BF16)

    sent = [[None] * RING, [None] * RING]
    forwarded = [[None] * RING, [None] * RING]

    def send_pair(i):
        rows = slice(32 * i, 32 * i + 32)
        for dc in range(2):
            if 2 * i + dc:
                routed[2 * i + dc].wait_recv()
        for way, (k, target) in enumerate(((1, right), (3, left))):
            copy = remote(own.at[rows, 0:LATE], ring.at[k - 1, rows, :], xss.at[way, i], xsr.at[way, i], e, target)
            copy.start()
            sent[way][i] = copy

    def forward_pair(i):
        for way, (k, target) in enumerate(((1, right), (3, left))):
            rows = slice(32 * i + 16 * way, 32 * i + 16 * way + 16)
            sent[way][i].wait_recv()
            copy = remote(ring.at[k - 1, rows, :], ring.at[1, rows, :], fws.at[way, i], fwr.at[way, i], e, target)
            copy.start()
            forwarded[way][i] = copy

    def hidden(g):
        rows = slice(g * ROWS_G, (g + 1) * ROWS_G)
        for i in range(g * PAIRS_G, (g + 1) * PAIRS_G):
            for way in range(2):
                forwarded[way][i].wait_recv()
        for j in range(max(1, g * 2 * PAIRS_G), (g + 1) * 2 * PAIRS_G):
            routed_early[j].wait_recv()

        def product(weights):
            total = dot_nt(own[rows, :], weights[0])
            for k in range(1, 4):
                total = total + dot_nt(ring[k - 1, rows, :], weights[k, :, 0:LATE])
                total = total + dot_nt(early[rows, (k - 1) * EARLY:k * EARLY], weights[k, :, LATE:WIDTH])
            return total

        gate = product(wgv)
        up = product(wuv)
        hid[rows, :] = (gate / (1.0 + jnp.exp(-gate)) * up).astype(BF16)

    far = [None] * GROUPS
    near = [None] * GROUPS

    def down(g, k, lanes=slice(0, LATE)):
        return dot_nn(hid[g * ROWS_G:(g + 1) * ROWS_G, :], wdv[k, :, lanes])

    def source_of(j):
        core = (c + j % 2) % 2
        u_s, v_s, su_s, sv_s = role(core)
        return u_s * su_s + ((v_s + RING - DV[j // 2]) % RING) * sv_s + core

    returned = [None] * 16
    returned_early = [None] * 16

    def send_back_early(g):
        rows = slice(g * ROWS_G, (g + 1) * ROWS_G)
        for k in range(1, 4):
            early_y[rows, (k - 1) * EARLY:k * EARLY] = down(g, k, slice(LATE, WIDTH)).astype(BF16)
        if g == 0:
            early_back[0:TOK, :] = early_y[0:TOK, :]
        for j in range(max(1, g * 2 * PAIRS_G), (g + 1) * 2 * PAIRS_G):
            copy = remote(early_y.at[rows_of(j), :], early_back.at[rows_of(j), :], eys.at[j], eyr.at[j], source_of(j), x)
            copy.start()
            returned_early[j] = copy

    def halves(way):
        return slice(way * HALF_G, (way + 1) * HALF_G), slice((1 - way) * HALF_G, (2 - way) * HALF_G)

    def send_far(g):
        a_out[g] = down(g, 2).astype(BF16)
        far[g] = []
        for way, target in enumerate((right, left)):
            copy = remote(a_out.at[g, halves(way)[0], :], a_in.at[way, g], ras.at[way, g], rar.at[way, g], e, target)
            copy.start()
            far[g].append(copy)

    def send_near(way, g, rows, late):
        target = left if way else right
        copy = remote(
            b_out.at[way, g, rows, :], b_in.at[way, g, rows, :],
            rbs.at[way, g, late], rbr.at[way, g, late], e, target,
        )
        copy.start()
        near[g].append(copy)

    def send_near_free(g):
        near[g] = []
        for way, k in enumerate((3, 1)):
            late, free = halves(way)
            term = down(g, k)
            b_late[way, g] = term[late, :]
            b_out[way, g, free, :] = term[free, :].astype(BF16)
            send_near(way, g, free, 0)

    def send_near_late(g):
        for way in range(2):
            late, _ = halves(way)
            far[g][way].wait_recv()
            b_out[way, g, late, :] = (b_late[way, g] + a_in[way, g].astype(F32)).astype(BF16)
            send_near(way, g, late, 1)

    def send_back(g):
        rows = slice(g * ROWS_G, (g + 1) * ROWS_G)
        term = down(g, 0)
        y_out[rows, LATE:WIDTH] = down(g, 0, slice(LATE, WIDTH)).astype(BF16)
        for copy in near[g]:
            copy.wait_recv()
        y_out[rows, 0:LATE] = (term + b_in[0, g].astype(F32) + b_in[1, g].astype(F32)).astype(BF16)
        if g == 0:
            back[0:TOK, :] = y_out[0:TOK, :]
        for j in range(max(1, g * 2 * PAIRS_G), (g + 1) * 2 * PAIRS_G):
            copy = remote(y_out.at[rows_of(j), :], back.at[rows_of(j), :], s3s.at[j], s3r.at[j], source_of(j), x)
            copy.start()
            returned[j] = copy

    summed_early = [None] * 3

    def send_sums_early():
        for copy in returned_early[1:]:
            copy.wait_recv()
        early_z[...] = (dot_nn(mix_hi[...], early_back[...]) + dot_nn(mix_lo[...], early_back[...])).astype(BF16)
        for k in (2, 1, 3):
            copy = remote(
                early_z.at[:, (k - 1) * EARLY:k * EARLY], early_sum.at[k - 1], ezs.at[k - 1], ezr.at[k - 1], e, (x + 4 - k) % 4
            )
            copy.start()
            summed_early[k - 1] = copy

    for i in range(RING):
        send_pair(i)
        if i >= LAG:
            forward_pair(i - LAG)
        if i == EARLY_AFTER:
            route_early()
    for copy in loads:
        copy.wait()
    hidden(0)
    for i in range(RING - LAG, RING):
        forward_pair(i)
    send_far(0)
    send_back_early(0)
    send_near_free(0)
    for g in range(1, GROUPS):
        hidden(g)
        send_far(g)
        send_back_early(g)
        send_near_late(g - 1)
        send_near_free(g)
        send_back(g - 1)
    send_near_late(GROUPS - 1)
    send_sums_early()
    send_back(GROUPS - 1)

    mixture = jnp.zeros((RING * TOK, WIDTH), F32)
    for g in range(GROUPS):
        rows = slice(g * ROWS_G, (g + 1) * ROWS_G)
        for j in range(g * 2 * PAIRS_G, (g + 1) * 2 * PAIRS_G):
            if j:
                returned[j].wait_recv()
        mixture = mixture + dot_nn(mix_hi[:, rows], back[rows, :]) + dot_nn(mix_lo[:, rows], back[rows, :])
    for copy in summed_early:
        copy.wait_recv()
    part = mixture[:, LATE:WIDTH] + early_sum[0].astype(F32) + early_sum[1].astype(F32) + early_sum[2].astype(F32)
    z_out[:, 0:LATE] = mixture[:, 0:LATE].astype(BF16)
    z_out[:, LATE:WIDTH] = part.astype(BF16)
    homes = []
    for du in FAR_FIRST:
        copy = remote(
            z_out.at[du * TOK:(du + 1) * TOK, :], z_in.at[du], s4s.at[du - 1], s4r.at[du - 1],
            ((u + RING - du) % RING) * su + v * sv + c, x,
        )
        copy.start()
        homes.append(copy)
    totals = [mixture[0:TOK, 0:LATE], part[0:TOK, :]]
    for du, copy in zip(FAR_FIRST, homes):
        copy.wait_recv()
        totals[0] = totals[0] + z_in[du, :, 0:LATE].astype(F32)
        totals[1] = totals[1] + z_in[du, :, LATE:WIDTH].astype(F32)
    out[:, 0:LATE] = totals[0].astype(BF16)
    out[:, LATE:WIDTH] = totals[1].astype(BF16)

    early_copies = crossing + routed_early[1:] + returned_early[1:] + summed_early
    for copy in gathers + routed[1:] + sum(sent + forwarded + far + near, []) + returned[1:] + homes + early_copies:
        copy.wait_send()


def per_device(tokens, routes, router_probs, w_gate, w_up, w_down):
    vmem = pl.BlockSpec(memory_space=pltpu.VMEM)
    hbm = pl.BlockSpec(memory_space=pltpu.HBM)
    dma = pltpu.SemaphoreType.DMA
    return pl.pallas_call(
        kernel,
        out_shape=jax.ShapeDtypeStruct((TOK, WIDTH), BF16),
        in_specs=[hbm] * 6,
        out_specs=vmem,
        scratch_shapes=[
            pltpu.VMEM((TOP, TOK), jnp.int32),
            pltpu.VMEM((TOP, TOK), F32),
            pltpu.VMEM((4, HID, WIDTH), BF16),
            pltpu.VMEM((4, HID, WIDTH), BF16),
            pltpu.VMEM((4, HID, WIDTH), BF16),
            pltpu.VMEM((TOK, 4 * EXPERTS), BF16),
            pltpu.VMEM((RING, TOK, MSG), BF16),
            pltpu.VMEM((RING * TOK, MSG), BF16),
            pltpu.VMEM((SLOTS, WIDTH), BF16),
            pltpu.VMEM((SLOTS, WIDTH), BF16),
            pltpu.VMEM((3, SLOTS, LATE), BF16),
            pltpu.VMEM((RING * TOK, SLOTS), BF16),
            pltpu.VMEM((RING * TOK, SLOTS), BF16),
            pltpu.VMEM((SLOTS, HID), BF16),
            pltpu.VMEM((GROUPS, ROWS_G, LATE), BF16),
            pltpu.VMEM((2, GROUPS, HALF_G, LATE), BF16),
            pltpu.VMEM((2, GROUPS, HALF_G, LATE), F32),
            pltpu.VMEM((2, GROUPS, ROWS_G, LATE), BF16),
            pltpu.VMEM((2, GROUPS, ROWS_G, LATE), BF16),
            pltpu.VMEM((SLOTS, WIDTH), BF16),
            pltpu.VMEM((SLOTS, WIDTH), BF16),
            pltpu.VMEM((RING * TOK, WIDTH), BF16),
            pltpu.VMEM((RING, TOK, WIDTH), BF16),
            pltpu.VMEM((RING * TOK, 3 * EARLY), BF16),
            pltpu.VMEM((SLOTS, 3 * EARLY), BF16),
            pltpu.VMEM((SLOTS, 3 * EARLY), BF16),
            pltpu.VMEM((SLOTS, 3 * EARLY), BF16),
            pltpu.VMEM((SLOTS, 3 * EARLY), BF16),
            pltpu.VMEM((RING * TOK, 3 * EARLY), BF16),
            pltpu.VMEM((3, RING * TOK, EARLY), BF16),
            dma((10,)),
            dma((12,)),
            dma((7,)), dma((7,)),
            dma((16,)), dma((16,)),
            dma((2, RING)), dma((2, RING)),
            dma((2, RING)), dma((2, RING)),
            dma((2, GROUPS)), dma((2, GROUPS)),
            dma((2, GROUPS, 2)), dma((2, GROUPS, 2)),
            dma((16,)), dma((16,)),
            dma((7,)), dma((7,)),
            dma((3,)), dma((3,)),
            dma((16,)), dma((16,)),
            dma((16,)), dma((16,)),
            dma((3,)), dma((3,)),
        ],
        compiler_params=pltpu.CompilerParams(
            collective_id=0, has_side_effects=True, vmem_limit_bytes=62 * 1024 * 1024
        ),
    )(tokens, routes.T, router_probs.T, w_gate, w_up, w_down)


def solution(mesh):
    in_specs = (
        P("expert", "pair"),
        P("expert", None),
        P("expert", None),
        P("expert", "pair", None),
        P("expert", "pair", None),
        P("expert", "pair", None),
    )
    out_specs = P("expert", "pair")
    return jax.shard_map(
        per_device, mesh=mesh, in_specs=in_specs, out_specs=out_specs, check_vma=False
    )
```

```python
import jax
import jax.numpy as jnp
from jax import lax
from jax.experimental import pallas as pl
from jax.experimental.pallas import tpu as pltpu
from jax.sharding import PartitionSpec as P

TOK = 16
TOP = 8
RING = 8
EXPERTS = 128
SLOTS = 256
WIDTH = 1024
HID = 192
DV = (0, 1, 7, 2, 6, 3, 5, 4)
GROUPS = 2
PAIRS_G = RING // GROUPS
ROWS_G = SLOTS // GROUPS
HALF_G = ROWS_G // 2
LAG = 2
EARLY_AFTER = 1
MSG = WIDTH + 128
EARLY_OUT = 384
LATE_OUT = WIDTH - EARLY_OUT
EARLY_BACK = 384
SPLIT = 640
PARTS = ((0, EARLY_BACK, WIDTH), (1, EARLY_BACK, SPLIT), (1, SPLIT, WIDTH))
FAR_FIRST = (4, 3, 5, 2, 6, 1, 7)
F32 = jnp.float32
BF16 = jnp.bfloat16


def dot_nt(a, b):
    return lax.dot_general(a, b, (((1,), (1,)), ((), ())), preferred_element_type=F32)


def dot_nn(a, b):
    return lax.dot_general(a, b, (((1,), (0,)), ((), ())), preferred_element_type=F32)


def iota(shape, dim):
    return lax.broadcasted_iota(jnp.int32, shape, dim)


def ones_where(condition):
    return jnp.where(condition, 1.0, 0.0).astype(BF16)


def kernel(
    tok_hbm, routes_hbm, probs_hbm, wg, wu, wd, out,
    routes, probs, wgv, wuv, wdv, pieces, snd, stg, outb, own, ring, mix_hi, mix_lo, hid,
    a_out, a_in, b_late, b_out, b_in, y_out, back, z_out, z_in, early_tok, early_out, early, early_y, early_back, early_z, early_in, early_send, early_sum,
    in_sem, w_sem, s1s, s1r, s2s, s2r, xss, xsr, fws, fwr, ras, rar, rbs, rbr, s3s, s3r, s4s, s4r,
    ets, etr, egs, egr, ers, err, eys, eyr, ehs, ehr, ezs, ezr,
):
    e = lax.axis_index("expert")
    x = lax.axis_index("pair")
    c = e % 2
    y = (e // 2) % RING
    z = e // (2 * RING)
    right = (x + 1) % 4
    left = (x + 3) % 4

    def role(core):
        u = (1 - core) * z + core * y
        v = (1 - core) * y + core * z
        return u, v, 16 - 14 * core, 2 + 14 * core

    u, v, su, sv = role(c)

    barrier = pltpu.get_barrier_semaphore()

    def greet(expert, pair):
        pl.semaphore_signal(barrier, inc=1, device_id=(expert, pair), device_id_type=pl.DeviceIdType.MESH)

    for d in FAR_FIRST:
        for core in range(2):
            greet(((z + d) % RING) * 16 + y * 2 + core, x)
            greet(z * 16 + ((y + d) % RING) * 2 + core, x)
    greet(z * 16 + y * 2 + (1 - c), x)
    for k in range(1, 4):
        greet(e, (x + k) % 4)

    inputs = [
        pltpu.make_async_copy(routes_hbm, routes, in_sem.at[8]),
        pltpu.make_async_copy(probs_hbm, probs, in_sem.at[9]),
        pltpu.make_async_copy(tok_hbm, stg.at[0:TOK, 0:WIDTH], in_sem.at[0]),
    ]
    for du in FAR_FIRST:
        inputs.append(pltpu.make_async_copy(tok_hbm, snd.at[du, :, 0:WIDTH], in_sem.at[du]))
    for copy in inputs:
        copy.start()

    loads = []
    for k in range(4):
        quarter = pl.ds(pl.multiple_of(((x + 4 - k) % 4) * WIDTH, WIDTH), WIDTH)
        for j, (src, dst) in enumerate(((wg, wgv), (wu, wuv), (wd, wdv))):
            copy = pltpu.make_async_copy(src.at[0, :, quarter], dst.at[k], w_sem.at[3 * k + j])
            copy.start()
            loads.append(copy)

    inputs[0].wait()
    inputs[1].wait()
    prob = probs[...]
    mixing = prob / jnp.sum(prob, axis=0, keepdims=True)
    chosen = routes[...]
    experts = iota((EXPERTS, TOK), 0)
    mix = jnp.zeros((EXPERTS, TOK), F32)
    for k in range(TOP):
        mix = jnp.where(chosen[k:k + 1, :] == experts, mixing[k:k + 1, :], mix)
    named = jnp.where(mix > 0, 1.0, 0.0).astype(BF16)
    row, col = iota((TOK, TOK), 0), iota((TOK, TOK), 1)
    second = dot_nn(named, ones_where(row < col)) > 0.5
    same_token = ones_where(row == col)
    for r in range(2):
        part = jnp.where(second, mix, 0.0) if r else jnp.where(second, 0.0, mix)
        high = part.astype(BF16)
        low = (part - high.astype(F32)).astype(BF16)
        for j, piece in enumerate((high, low)):
            start = (2 * j + r) * EXPERTS
            pieces[:, start:start + EXPERTS] = dot_nt(same_token, piece).astype(BF16)
    lane = iota((RING * 128, 1), 0)
    pair = (lane >> 2) & 7
    offset = jnp.where((pair & 1) == 1, (pair + 1) >> 1, (8 - (pair >> 1)) & 7)
    owner = ((u + (lane >> 7)) & 7) * su + ((v + offset) & 7) * sv + ((c + (lane >> 1)) & 1)
    column = ((lane >> 5) & 3) * 2 * EXPERTS + (lane & 1) * EXPERTS + owner
    pick = ones_where(iota((RING * 128, 4 * EXPERTS), 1) == column)
    blocks = dot_nt(pieces[...], pick).astype(BF16)
    stg[0:TOK, WIDTH:MSG] = blocks[:, 0:128]
    for du in range(1, RING):
        snd[du, :, WIDTH:MSG] = blocks[:, du * 128:(du + 1) * 128]
    for copy in inputs[2:]:
        copy.wait()

    pl.semaphore_wait(barrier, 32)

    def remote(src, dst, send, recv, expert, pair):
        return pltpu.make_async_remote_copy(
            src_ref=src, dst_ref=dst, send_sem=send, recv_sem=recv,
            device_id=(expert, pair), device_id_type=pl.DeviceIdType.MESH,
        )

    crossing = [None] * 3
    for k in (2, 1, 3):
        copy = remote(
            stg.at[0:TOK, LATE_OUT:WIDTH], early_tok.at[0:TOK, (k - 1) * EARLY_OUT:k * EARLY_OUT],
            ets.at[k - 1], etr.at[k - 1], e, (x + k) % 4,
        )
        copy.start()
        crossing[k - 1] = copy
    gathers, gathers_early = [], []
    for du in FAR_FIRST:
        copy = remote(
            snd.at[du], stg.at[du * TOK:(du + 1) * TOK, :], s1s.at[du - 1], s1r.at[du - 1],
            ((u + du) % RING) * su + v * sv + c, x,
        )
        copy.start()
        gathers.append(copy)
    slot = iota((SLOTS, 128), 0)
    spread = [ones_where(iota((SLOTS, 128), 1) == 32 * j + ((slot >> 4) << 1) + (slot & 1)) for j in range(2)]
    for copy in crossing:
        copy.wait_recv()
    for du in FAR_FIRST:
        copy = remote(
            early_tok.at[0:TOK, :], early_tok.at[du * TOK:(du + 1) * TOK, :], egs.at[du - 1], egr.at[du - 1],
            ((u + du) % RING) * su + v * sv + c, x,
        )
        copy.start()
        gathers_early.append(copy)
    for copy in gathers:
        copy.wait_recv()

    source = stg[:, WIDTH:MSG]
    tok_du = iota((SLOTS, RING * TOK), 1) >> 4
    slot_du = (iota((SLOTS, RING * TOK), 0) >> 1) & 7
    placing = ones_where(jnp.logical_and(dot_nt(spread[0], source) > 0, tok_du == slot_du))
    routed = [None] * 16
    routed_early = [None] * 16

    def owner_of(j):
        return u * su + ((v + DV[j // 2]) % RING) * sv + (c + j % 2) % 2

    def rows_of(j):
        return slice(j * 16, (j + 1) * 16)

    def route_early():
        for copy in gathers_early:
            copy.wait_recv()
        early_out[...] = dot_nn(placing, early_tok[...]).astype(BF16)
        early[0:TOK, :] = early_out[0:TOK, :]
        for j in range(1, 16):
            copy = remote(early_out.at[rows_of(j), :], early.at[rows_of(j), :], ers.at[j], err.at[j], owner_of(j), x)
            copy.start()
            routed_early[j] = copy

    for g in range(GROUPS):
        rows = dot_nn(placing[g * ROWS_G:(g + 1) * ROWS_G, :], stg[:, 0:WIDTH]).astype(BF16)
        outb[g * ROWS_G:(g + 1) * ROWS_G, :] = rows
        if g == 0:
            own[0:TOK, :] = rows[0:TOK, :]
        for j in range(max(1, g * 2 * PAIRS_G), (g + 1) * 2 * PAIRS_G):
            copy = remote(outb.at[rows_of(j), :], own.at[rows_of(j), :], s2s.at[j], s2r.at[j], owner_of(j), x)
            copy.start()
            routed[j] = copy

    tok_du = iota((RING * TOK, SLOTS), 0) >> 4
    slot_du = (iota((RING * TOK, SLOTS), 1) >> 1) & 7
    same = tok_du == slot_du
    mix_hi[...] = jnp.where(same, dot_nt(source, spread[0]), 0.0).astype(BF16)
    mix_lo[...] = jnp.where(same, dot_nt(source, spread[1]), 0.0).astype(BF16)

    sent = [[None] * RING, [None] * RING]
    forwarded = [[None] * RING, [None] * RING]

    def send_pair(i):
        rows = slice(32 * i, 32 * i + 32)
        for dc in range(2):
            if 2 * i + dc:
                routed[2 * i + dc].wait_recv()
        for way, (k, target) in enumerate(((1, right), (3, left))):
            copy = remote(own.at[rows, 0:LATE_OUT], ring.at[k - 1, rows, :], xss.at[way, i], xsr.at[way, i], e, target)
            copy.start()
            sent[way][i] = copy

    def forward_pair(i):
        for way, (k, target) in enumerate(((1, right), (3, left))):
            rows = slice(32 * i + 16 * way, 32 * i + 16 * way + 16)
            sent[way][i].wait_recv()
            copy = remote(ring.at[k - 1, rows, :], ring.at[1, rows, :], fws.at[way, i], fwr.at[way, i], e, target)
            copy.start()
            forwarded[way][i] = copy

    def hidden(g):
        rows = slice(g * ROWS_G, (g + 1) * ROWS_G)
        pairs = range(g * PAIRS_G, (g + 1) * PAIRS_G)
        weights = (wgv, wuv)
        totals = [dot_nt(own[rows, :], w[0]) for w in weights]
        for way, k in enumerate((1, 3)):
            totals = [t + dot_nt(ring[k - 1, rows, :], w[k, :, 0:LATE_OUT]) for t, w in zip(totals, weights)]
        for i in pairs:
            for j in (2 * i, 2 * i + 1):
                if j:
                    routed_early[j].wait_recv()
        for k in range(1, 4):
            lanes = slice((k - 1) * EARLY_OUT, k * EARLY_OUT)
            totals = [t + dot_nt(early[rows, lanes], w[k, :, LATE_OUT:WIDTH]) for t, w in zip(totals, weights)]
        for i in pairs:
            for way in range(2):
                forwarded[way][i].wait_recv()
        gate, up = [t + dot_nt(ring[1, rows, :], w[2, :, 0:LATE_OUT]) for t, w in zip(totals, weights)]
        hid[rows, :] = (gate / (1.0 + jnp.exp(-gate)) * up).astype(BF16)

    far = [None] * len(PARTS)
    near = [None] * len(PARTS)

    def down(g, k, lanes):
        return dot_nn(hid[g * ROWS_G:(g + 1) * ROWS_G, :], wdv[k, :, lanes])

    def source_of(j):
        core = (c + j % 2) % 2
        u_s, v_s, su_s, sv_s = role(core)
        return u_s * su_s + ((v_s + RING - DV[j // 2]) % RING) * sv_s + core

    returned = [None] * len(PARTS)
    returned_early = [None] * 16

    def send_back_early(g):
        rows = slice(g * ROWS_G, (g + 1) * ROWS_G)
        for k in range(1, 4):
            early_y[rows, (k - 1) * EARLY_BACK:k * EARLY_BACK] = down(g, k, slice(0, EARLY_BACK)).astype(BF16)
        if g == 0:
            early_back[0:TOK, :] = early_y[0:TOK, :]
        for j in range(max(1, g * 2 * PAIRS_G), (g + 1) * 2 * PAIRS_G):
            copy = remote(early_y.at[rows_of(j), :], early_back.at[rows_of(j), :], eys.at[j], eyr.at[j], source_of(j), x)
            copy.start()
            returned_early[j] = copy

    def halves(way):
        return slice(way * HALF_G, (way + 1) * HALF_G), slice((1 - way) * HALF_G, (2 - way) * HALF_G)

    def send_far(p):
        g, first, last = PARTS[p]
        lanes = slice(first, last)
        a_out[g, :, lanes] = down(g, 2, lanes).astype(BF16)
        far[p] = []
        for way, target in enumerate((right, left)):
            copy = remote(
                a_out.at[g, halves(way)[0], lanes], a_in.at[way, g, :, lanes], ras.at[way, p], rar.at[way, p], e, target
            )
            copy.start()
            far[p].append(copy)

    def send_near(way, p, rows, late):
        g, first, last = PARTS[p]
        copy = remote(
            b_out.at[way, g, rows, first:last], b_in.at[way, g, rows, first:last],
            rbs.at[way, p, late], rbr.at[way, p, late], e, left if way else right,
        )
        copy.start()
        near[p].append(copy)

    def send_near_free(p):
        g, first, last = PARTS[p]
        near[p] = []
        for way, k in enumerate((3, 1)):
            late, free = halves(way)
            term = down(g, k, slice(first, last))
            b_late[way, g, :, first:last] = term[late, :]
            b_out[way, g, free, first:last] = term[free, :].astype(BF16)
            send_near(way, p, free, 0)

    def send_near_late(p):
        g, first, last = PARTS[p]
        lanes = slice(first, last)
        for way in range(2):
            late, _ = halves(way)
            far[p][way].wait_recv()
            b_out[way, g, late, lanes] = (b_late[way, g, :, lanes] + a_in[way, g, :, lanes].astype(F32)).astype(BF16)
            send_near(way, p, late, 1)

    def send_back(p):
        g, first, last = PARTS[p]
        rows = slice(g * ROWS_G, (g + 1) * ROWS_G)
        lanes = slice(first, last)
        term = down(g, 0, lanes)
        start = first
        if first == EARLY_BACK:
            start = 0
            y_out[rows, 0:EARLY_BACK] = down(g, 0, slice(0, EARLY_BACK)).astype(BF16)
        for copy in near[p]:
            copy.wait_recv()
        y_out[rows, lanes] = (term + b_in[0, g, :, lanes].astype(F32) + b_in[1, g, :, lanes].astype(F32)).astype(BF16)
        if g == 0:
            back[0:TOK, :] = y_out[0:TOK, :]
        returned[p] = []
        for j in range(max(1, g * 2 * PAIRS_G), (g + 1) * 2 * PAIRS_G):
            copy = remote(
                y_out.at[rows_of(j), start:last], back.at[rows_of(j), start:last], s3s.at[p, j], s3r.at[p, j], source_of(j), x
            )
            copy.start()
            returned[p].append(copy)

    def home_of(du):
        return ((u + RING - du) % RING) * su + v * sv + c

    homes_early, homes = [], []
    summed_early = [None] * 3

    def send_home_early():
        for copy in returned_early[1:]:
            copy.wait_recv()
        sums = dot_nn(mix_hi[...], early_back[...]) + dot_nn(mix_lo[...], early_back[...])
        early_z[...] = sums.astype(BF16)
        for du in FAR_FIRST:
            copy = remote(early_z.at[du * TOK:(du + 1) * TOK, :], early_in.at[du], ehs.at[du - 1], ehr.at[du - 1], home_of(du), x)
            copy.start()
            homes_early.append(copy)
        return sums[0:TOK, :]

    def send_sums_early(sums):
        for du, copy in zip(FAR_FIRST, homes_early):
            copy.wait_recv()
            sums = sums + early_in[du].astype(F32)
        early_send[...] = sums.astype(BF16)
        for k in (2, 1, 3):
            copy = remote(
                early_send.at[:, (k - 1) * EARLY_BACK:k * EARLY_BACK], early_sum.at[k - 1],
                ezs.at[k - 1], ezr.at[k - 1], e, (x + 4 - k) % 4,
            )
            copy.start()
            summed_early[k - 1] = copy

    for i in range(RING):
        send_pair(i)
        if i >= LAG:
            forward_pair(i - LAG)
        if i == EARLY_AFTER:
            route_early()
    for copy in loads:
        copy.wait()
    hidden(0)
    for i in range(RING - LAG, RING):
        forward_pair(i)
    send_far(0)
    send_near_free(0)
    send_back_early(0)
    hidden(1)
    send_far(1)
    send_far(2)
    send_near_late(0)
    send_back_early(1)
    send_near_free(1)
    send_near_free(2)
    send_near_late(1)
    send_near_late(2)
    send_back(0)

    send_back(1)
    send_back(2)
    sums_early = send_home_early()
    halves_home = []
    for h, (start, last) in enumerate(((0, SPLIT), (SPLIT, WIDTH))):
        for copy in (returned[0] if h == 0 else []) + returned[1 + h]:
            copy.wait_recv()
        mixture = dot_nn(mix_hi[...], back[:, start:last]) + dot_nn(mix_lo[...], back[:, start:last])
        z_out[:, start:last] = mixture.astype(BF16)
        for du in FAR_FIRST:
            copy = remote(
                z_out.at[du * TOK:(du + 1) * TOK, start:last], z_in.at[du, :, start:last],
                s4s.at[h, du - 1], s4r.at[h, du - 1], home_of(du), x,
            )
            copy.start()
            homes.append(copy)
        halves_home.append(mixture[0:TOK, :])
    send_sums_early(sums_early)
    for h, (start, last) in enumerate(((0, SPLIT), (SPLIT, WIDTH))):
        total = halves_home[h]
        for du, copy in zip(FAR_FIRST, homes[7 * h:]):
            copy.wait_recv()
            total = total + z_in[du, :, start:last].astype(F32)
        if h == 0:
            part = total[:, 0:EARLY_BACK]
            out[:, EARLY_BACK:SPLIT] = total[:, EARLY_BACK:SPLIT].astype(BF16)
        else:
            out[:, SPLIT:WIDTH] = total.astype(BF16)
    for k, copy in enumerate(summed_early):
        copy.wait_recv()
        part = part + early_sum[k].astype(F32)
    out[:, 0:EARLY_BACK] = part.astype(BF16)

    early_copies = crossing + gathers_early + routed_early[1:] + returned_early[1:] + homes_early + summed_early
    for copy in gathers + routed[1:] + sum(sent + forwarded + far + near + returned, []) + homes + early_copies:
        copy.wait_send()


def per_device(tokens, routes, router_probs, w_gate, w_up, w_down):
    vmem = pl.BlockSpec(memory_space=pltpu.VMEM)
    hbm = pl.BlockSpec(memory_space=pltpu.HBM)
    dma = pltpu.SemaphoreType.DMA
    return pl.pallas_call(
        kernel,
        out_shape=jax.ShapeDtypeStruct((TOK, WIDTH), BF16),
        in_specs=[hbm] * 6,
        out_specs=vmem,
        scratch_shapes=[
            pltpu.VMEM((TOP, TOK), jnp.int32),
            pltpu.VMEM((TOP, TOK), F32),
            pltpu.VMEM((4, HID, WIDTH), BF16),
            pltpu.VMEM((4, HID, WIDTH), BF16),
            pltpu.VMEM((4, HID, WIDTH), BF16),
            pltpu.VMEM((TOK, 4 * EXPERTS), BF16),
            pltpu.VMEM((RING, TOK, MSG), BF16),
            pltpu.VMEM((RING * TOK, MSG), BF16),
            pltpu.VMEM((SLOTS, WIDTH), BF16),
            pltpu.VMEM((SLOTS, WIDTH), BF16),
            pltpu.VMEM((3, SLOTS, LATE_OUT), BF16),
            pltpu.VMEM((RING * TOK, SLOTS), BF16),
            pltpu.VMEM((RING * TOK, SLOTS), BF16),
            pltpu.VMEM((SLOTS, HID), BF16),
            pltpu.VMEM((GROUPS, ROWS_G, WIDTH), BF16),
            pltpu.VMEM((2, GROUPS, HALF_G, WIDTH), BF16),
            pltpu.VMEM((2, GROUPS, HALF_G, WIDTH), F32),
            pltpu.VMEM((2, GROUPS, ROWS_G, WIDTH), BF16),
            pltpu.VMEM((2, GROUPS, ROWS_G, WIDTH), BF16),
            pltpu.VMEM((SLOTS, WIDTH), BF16),
            pltpu.VMEM((SLOTS, WIDTH), BF16),
            pltpu.VMEM((RING * TOK, WIDTH), BF16),
            pltpu.VMEM((RING, TOK, WIDTH), BF16),
            pltpu.VMEM((RING * TOK, 3 * EARLY_OUT), BF16),
            pltpu.VMEM((SLOTS, 3 * EARLY_OUT), BF16),
            pltpu.VMEM((SLOTS, 3 * EARLY_OUT), BF16),
            pltpu.VMEM((SLOTS, 3 * EARLY_BACK), BF16),
            pltpu.VMEM((SLOTS, 3 * EARLY_BACK), BF16),
            pltpu.VMEM((RING * TOK, 3 * EARLY_BACK), BF16),
            pltpu.VMEM((RING, TOK, 3 * EARLY_BACK), BF16),
            pltpu.VMEM((TOK, 3 * EARLY_BACK), BF16),
            pltpu.VMEM((3, TOK, EARLY_BACK), BF16),
            dma((10,)),
            dma((12,)),
            dma((7,)), dma((7,)),
            dma((16,)), dma((16,)),
            dma((2, RING)), dma((2, RING)),
            dma((2, RING)), dma((2, RING)),
            dma((2, len(PARTS))), dma((2, len(PARTS))),
            dma((2, len(PARTS), 2)), dma((2, len(PARTS), 2)),
            dma((len(PARTS), 16)), dma((len(PARTS), 16)),
            dma((2, 7)), dma((2, 7)),
            dma((3,)), dma((3,)),
            dma((7,)), dma((7,)),
            dma((16,)), dma((16,)),
            dma((16,)), dma((16,)),
            dma((7,)), dma((7,)),
            dma((3,)), dma((3,)),
        ],
        compiler_params=pltpu.CompilerParams(
            collective_id=0, has_side_effects=True, vmem_limit_bytes=40 * 1024 * 1024
        ),
    )(*(
        pltpu.with_memory_space_constraint(a, pltpu.HBM)
        for a in (tokens, routes.T, router_probs.T, w_gate, w_up, w_down)
    ))


def solution(mesh):
    in_specs = (
        P("expert", "pair"),
        P("expert", None),
        P("expert", None),
        P("expert", "pair", None),
        P("expert", "pair", None),
        P("expert", "pair", None),
    )
    out_specs = P("expert", "pair")
    return jax.shard_map(
        per_device, mesh=mesh, in_specs=in_specs, out_specs=out_specs, check_vma=False
    )
```

```python
import jax
import jax.numpy as jnp
from jax import lax
from jax.experimental import pallas as pl
from jax.experimental.pallas import tpu as pltpu
from jax.sharding import PartitionSpec as P

TOK = 16
TOP = 8
RING = 8
EXPERTS = 128
SLOTS = 256
WIDTH = 1024
HID = 192
DV = (0, 1, 7, 2, 6, 3, 5, 4)
GROUPS = 2
PAIRS_G = RING // GROUPS
ROWS_G = SLOTS // GROUPS
HALF_G = ROWS_G // 2
LAG = 3
EARLY_AFTER = 1
MSG = WIDTH + 128
EARLY_OUT = 384
LATE_OUT = WIDTH - EARLY_OUT
EARLY_BACK = 384
SPLIT = 512
PARTS = ((0, EARLY_BACK, WIDTH), (1, EARLY_BACK, SPLIT), (1, SPLIT, WIDTH))
FAR_FIRST = (4, 3, 5, 2, 6, 1, 7)
F32 = jnp.float32
BF16 = jnp.bfloat16


def dot_nt(a, b):
    return lax.dot_general(a, b, (((1,), (1,)), ((), ())), preferred_element_type=F32)


def dot_nn(a, b):
    return lax.dot_general(a, b, (((1,), (0,)), ((), ())), preferred_element_type=F32)


def iota(shape, dim):
    return lax.broadcasted_iota(jnp.int32, shape, dim)


def ones_where(condition):
    return jnp.where(condition, 1.0, 0.0).astype(BF16)


def kernel(
    tok_hbm, routes_hbm, probs_hbm, wg, wu, wd, out,
    routes, probs, wgv, wuv, wdv, pick, snd, stg, outb, own, ring, mix_hi, mix_lo, hid,
    a_out, a_in, b_late, b_out, b_in, y_out, back, z_out, z_in, early_tok, early_out, early, early_y, early_back, early_z, early_in, early_send, early_sum,
    in_sem, w_sem, s1s, s1r, sbs, sbr, s2s, s2r, xss, xsr, fws, fwr, ras, rar, rbs, rbr, s3s, s3r, s4s, s4r,
    ets, etr, egs, egr, ers, err, eys, eyr, ehs, ehr, ezs, ezr,
):
    e = lax.axis_index("expert")
    x = lax.axis_index("pair")
    c = e % 2
    y = (e // 2) % RING
    z = e // (2 * RING)
    right = (x + 1) % 4
    left = (x + 3) % 4

    def role(core):
        u = (1 - core) * z + core * y
        v = (1 - core) * y + core * z
        return u, v, 16 - 14 * core, 2 + 14 * core

    u, v, su, sv = role(c)

    barrier = pltpu.get_barrier_semaphore()

    def greet(expert, pair):
        pl.semaphore_signal(barrier, inc=1, device_id=(expert, pair), device_id_type=pl.DeviceIdType.MESH)

    for d in FAR_FIRST:
        for core in range(2):
            greet(((z + d) % RING) * 16 + y * 2 + core, x)
            greet(z * 16 + ((y + d) % RING) * 2 + core, x)
    greet(z * 16 + y * 2 + (1 - c), x)
    for k in range(1, 4):
        greet(e, (x + k) % 4)

    inputs = [
        pltpu.make_async_copy(routes_hbm, routes, in_sem.at[1]),
        pltpu.make_async_copy(probs_hbm, probs, in_sem.at[2]),
        pltpu.make_async_copy(tok_hbm, stg.at[0:TOK, 0:WIDTH], in_sem.at[0]),
    ]
    for copy in inputs:
        copy.start()

    loads = []
    for k in range(4):
        quarter = pl.ds(pl.multiple_of(((x + 4 - k) % 4) * WIDTH, WIDTH), WIDTH)
        for j, (src, dst) in enumerate(((wg, wgv), (wu, wuv), (wd, wdv))):
            copy = pltpu.make_async_copy(src.at[0, :, quarter], dst.at[k], w_sem.at[3 * k + j])
            copy.start()
            loads.append(copy)

    lane = iota((RING * 128, 1), 0)
    pair = (lane >> 2) & 7
    offset = jnp.where((pair & 1) == 1, (pair + 1) >> 1, (8 - (pair >> 1)) & 7)
    owner = ((u + (lane >> 7)) & 7) * su + ((v + offset) & 7) * sv + ((c + (lane >> 1)) & 1)
    column = ((lane >> 5) & 3) * 2 * EXPERTS + (lane & 1) * EXPERTS + owner
    pick[...] = ones_where(iota((RING * 128, 4 * EXPERTS), 1) == column)

    inputs[2].wait()
    pl.semaphore_wait(barrier, 32)

    def remote(src, dst, send, recv, expert, pair):
        return pltpu.make_async_remote_copy(
            src_ref=src, dst_ref=dst, send_sem=send, recv_sem=recv,
            device_id=(expert, pair), device_id_type=pl.DeviceIdType.MESH,
        )

    crossing = [None] * 3
    for k in (2, 1, 3):
        copy = remote(
            stg.at[0:TOK, LATE_OUT:WIDTH], early_tok.at[0:TOK, (k - 1) * EARLY_OUT:k * EARLY_OUT],
            ets.at[k - 1], etr.at[k - 1], e, (x + k) % 4,
        )
        copy.start()
        crossing[k - 1] = copy

    def peer_of(du):
        return ((u + du) % RING) * su + v * sv + c

    gathers, gathers_early = [], []
    for du in FAR_FIRST:
        copy = remote(
            stg.at[0:TOK, 0:WIDTH], stg.at[du * TOK:(du + 1) * TOK, 0:WIDTH], s1s.at[du - 1], s1r.at[du - 1], peer_of(du), x
        )
        copy.start()
        gathers.append(copy)

    inputs[0].wait()
    inputs[1].wait()
    prob = probs[...]
    mixing = prob / jnp.sum(prob, axis=0, keepdims=True)
    chosen = routes[...]
    experts = iota((EXPERTS, TOK), 0)
    mix = jnp.zeros((EXPERTS, TOK), F32)
    for k in range(TOP):
        mix = jnp.where(chosen[k:k + 1, :] == experts, mixing[k:k + 1, :], mix)
    named = jnp.where(mix > 0, 1.0, 0.0).astype(BF16)
    row, col = iota((TOK, TOK), 0), iota((TOK, TOK), 1)
    second = dot_nn(named, ones_where(row < col)) > 0.5
    same_token = ones_where(row == col)
    parts = [jnp.where(second, 0.0, mix), jnp.where(second, mix, 0.0)]
    pieces = [part.astype(BF16) for part in parts]
    pieces += [(part - high.astype(F32)).astype(BF16) for part, high in zip(parts, pieces)]
    blocks = dot_nt(dot_nt(same_token, jnp.concatenate(pieces, axis=0)).astype(BF16), pick[...]).astype(BF16)
    stg[0:TOK, WIDTH:MSG] = blocks[:, 0:128]
    for du in FAR_FIRST:
        snd[du] = blocks[:, du * 128:(du + 1) * 128]
        copy = remote(
            snd.at[du], stg.at[du * TOK:(du + 1) * TOK, WIDTH:MSG], sbs.at[du - 1], sbr.at[du - 1], peer_of(du), x
        )
        copy.start()
        gathers.append(copy)

    slot = iota((SLOTS, 128), 0)
    spread = [ones_where(iota((SLOTS, 128), 1) == 32 * j + ((slot >> 4) << 1) + (slot & 1)) for j in range(2)]
    for copy in crossing:
        copy.wait_recv()
    for du in FAR_FIRST:
        copy = remote(
            early_tok.at[0:TOK, :], early_tok.at[du * TOK:(du + 1) * TOK, :], egs.at[du - 1], egr.at[du - 1],
            peer_of(du), x,
        )
        copy.start()
        gathers_early.append(copy)
    for copy in gathers:
        copy.wait_recv()

    source = stg[:, WIDTH:MSG]
    tok_du = iota((SLOTS, RING * TOK), 1) >> 4
    slot_du = (iota((SLOTS, RING * TOK), 0) >> 1) & 7
    placing = ones_where(jnp.logical_and(dot_nt(spread[0], source) > 0, tok_du == slot_du))
    routed = [None] * 16
    routed_early = [None] * 16

    def owner_of(j):
        return u * su + ((v + DV[j // 2]) % RING) * sv + (c + j % 2) % 2

    def rows_of(j):
        return slice(j * 16, (j + 1) * 16)

    def route_early():
        for copy in gathers_early:
            copy.wait_recv()
        early_out[...] = dot_nn(placing, early_tok[...]).astype(BF16)
        early[0:TOK, :] = early_out[0:TOK, :]
        for j in range(1, 16):
            copy = remote(early_out.at[rows_of(j), :], early.at[rows_of(j), :], ers.at[j], err.at[j], owner_of(j), x)
            copy.start()
            routed_early[j] = copy

    for g in range(GROUPS):
        rows = dot_nn(placing[g * ROWS_G:(g + 1) * ROWS_G, :], stg[:, 0:WIDTH]).astype(BF16)
        outb[g * ROWS_G:(g + 1) * ROWS_G, :] = rows
        if g == 0:
            own[0:TOK, :] = rows[0:TOK, :]
        for j in range(max(1, g * 2 * PAIRS_G), (g + 1) * 2 * PAIRS_G):
            copy = remote(outb.at[rows_of(j), :], own.at[rows_of(j), :], s2s.at[j], s2r.at[j], owner_of(j), x)
            copy.start()
            routed[j] = copy

    tok_du = iota((RING * TOK, SLOTS), 0) >> 4
    slot_du = (iota((RING * TOK, SLOTS), 1) >> 1) & 7
    same = tok_du == slot_du
    mix_hi[...] = jnp.where(same, dot_nt(source, spread[0]), 0.0).astype(BF16)
    mix_lo[...] = jnp.where(same, dot_nt(source, spread[1]), 0.0).astype(BF16)

    sent = [[None] * RING, [None] * RING]
    forwarded = [[None] * RING, [None] * RING]

    def send_pair(i):
        rows = slice(32 * i, 32 * i + 32)
        for dc in range(2):
            if 2 * i + dc:
                routed[2 * i + dc].wait_recv()
        for way, (k, target) in enumerate(((1, right), (3, left))):
            copy = remote(own.at[rows, 0:LATE_OUT], ring.at[k - 1, rows, :], xss.at[way, i], xsr.at[way, i], e, target)
            copy.start()
            sent[way][i] = copy

    def forward_pair(i):
        for way, (k, target) in enumerate(((1, right), (3, left))):
            rows = slice(32 * i + 16 * way, 32 * i + 16 * way + 16)
            sent[way][i].wait_recv()
            copy = remote(ring.at[k - 1, rows, :], ring.at[1, rows, :], fws.at[way, i], fwr.at[way, i], e, target)
            copy.start()
            forwarded[way][i] = copy

    def hidden(g):
        rows = slice(g * ROWS_G, (g + 1) * ROWS_G)
        pairs = range(g * PAIRS_G, (g + 1) * PAIRS_G)
        weights = (wgv, wuv)
        totals = [dot_nt(own[rows, :], w[0]) for w in weights]
        for way, k in enumerate((1, 3)):
            totals = [t + dot_nt(ring[k - 1, rows, :], w[k, :, 0:LATE_OUT]) for t, w in zip(totals, weights)]
        for i in pairs:
            for j in (2 * i, 2 * i + 1):
                if j:
                    routed_early[j].wait_recv()
        for k in range(1, 4):
            lanes = slice((k - 1) * EARLY_OUT, k * EARLY_OUT)
            totals = [t + dot_nt(early[rows, lanes], w[k, :, LATE_OUT:WIDTH]) for t, w in zip(totals, weights)]
        for i in pairs:
            for way in range(2):
                forwarded[way][i].wait_recv()
        gate, up = [t + dot_nt(ring[1, rows, :], w[2, :, 0:LATE_OUT]) for t, w in zip(totals, weights)]
        hid[rows, :] = (gate / (1.0 + jnp.exp(-gate)) * up).astype(BF16)

    far = [None] * len(PARTS)
    near = [None] * len(PARTS)

    def down(g, k, lanes):
        return dot_nn(hid[g * ROWS_G:(g + 1) * ROWS_G, :], wdv[k, :, lanes])

    def source_of(j):
        core = (c + j % 2) % 2
        u_s, v_s, su_s, sv_s = role(core)
        return u_s * su_s + ((v_s + RING - DV[j // 2]) % RING) * sv_s + core

    returned = [None] * len(PARTS)
    returned_early = [None] * 16

    def send_back_early(g):
        rows = slice(g * ROWS_G, (g + 1) * ROWS_G)
        for k in range(1, 4):
            early_y[rows, (k - 1) * EARLY_BACK:k * EARLY_BACK] = down(g, k, slice(0, EARLY_BACK)).astype(BF16)
        if g == 0:
            early_back[0:TOK, :] = early_y[0:TOK, :]
        for j in range(max(1, g * 2 * PAIRS_G), (g + 1) * 2 * PAIRS_G):
            copy = remote(early_y.at[rows_of(j), :], early_back.at[rows_of(j), :], eys.at[j], eyr.at[j], source_of(j), x)
            copy.start()
            returned_early[j] = copy

    def halves(way):
        return slice(way * HALF_G, (way + 1) * HALF_G), slice((1 - way) * HALF_G, (2 - way) * HALF_G)

    def send_far(p):
        g, first, last = PARTS[p]
        lanes = slice(first, last)
        a_out[g, :, lanes] = down(g, 2, lanes).astype(BF16)
        far[p] = []
        for way, target in enumerate((right, left)):
            copy = remote(
                a_out.at[g, halves(way)[0], lanes], a_in.at[way, g, :, lanes], ras.at[way, p], rar.at[way, p], e, target
            )
            copy.start()
            far[p].append(copy)

    def send_near(way, p, rows, late):
        g, first, last = PARTS[p]
        copy = remote(
            b_out.at[way, g, rows, first:last], b_in.at[way, g, rows, first:last],
            rbs.at[way, p, late], rbr.at[way, p, late], e, left if way else right,
        )
        copy.start()
        near[p].append(copy)

    def send_near_free(p):
        g, first, last = PARTS[p]
        near[p] = []
        for way, k in enumerate((3, 1)):
            late, free = halves(way)
            term = down(g, k, slice(first, last))
            b_late[way, g, :, first:last] = term[late, :]
            b_out[way, g, free, first:last] = term[free, :].astype(BF16)
            send_near(way, p, free, 0)

    def send_near_late(p):
        g, first, last = PARTS[p]
        lanes = slice(first, last)
        for way in range(2):
            late, _ = halves(way)
            far[p][way].wait_recv()
            b_out[way, g, late, lanes] = (b_late[way, g, :, lanes] + a_in[way, g, :, lanes].astype(F32)).astype(BF16)
            send_near(way, p, late, 1)

    def send_back(p):
        g, first, last = PARTS[p]
        rows = slice(g * ROWS_G, (g + 1) * ROWS_G)
        lanes = slice(first, last)
        term = down(g, 0, lanes)
        start = first
        if first == EARLY_BACK:
            start = 0
            y_out[rows, 0:EARLY_BACK] = down(g, 0, slice(0, EARLY_BACK)).astype(BF16)
        for copy in near[p]:
            copy.wait_recv()
        y_out[rows, lanes] = (term + b_in[0, g, :, lanes].astype(F32) + b_in[1, g, :, lanes].astype(F32)).astype(BF16)
        if g == 0:
            back[0:TOK, :] = y_out[0:TOK, :]
        returned[p] = []
        for j in range(max(1, g * 2 * PAIRS_G), (g + 1) * 2 * PAIRS_G):
            copy = remote(
                y_out.at[rows_of(j), start:last], back.at[rows_of(j), start:last], s3s.at[p, j], s3r.at[p, j], source_of(j), x
            )
            copy.start()
            returned[p].append(copy)

    def home_of(du):
        return ((u + RING - du) % RING) * su + v * sv + c

    homes_early, homes = [], []
    summed_early = [None] * 3

    def send_home_early():
        for copy in returned_early[1:]:
            copy.wait_recv()
        sums = dot_nn(mix_hi[...], early_back[...]) + dot_nn(mix_lo[...], early_back[...])
        early_z[...] = sums.astype(BF16)
        for du in FAR_FIRST:
            copy = remote(early_z.at[du * TOK:(du + 1) * TOK, :], early_in.at[du], ehs.at[du - 1], ehr.at[du - 1], home_of(du), x)
            copy.start()
            homes_early.append(copy)
        return sums[0:TOK, :]

    def send_sums_early(sums):
        for du, copy in zip(FAR_FIRST, homes_early):
            copy.wait_recv()
            sums = sums + early_in[du].astype(F32)
        early_send[...] = sums.astype(BF16)
        for k in (2, 1, 3):
            copy = remote(
                early_send.at[:, (k - 1) * EARLY_BACK:k * EARLY_BACK], early_sum.at[k - 1],
                ezs.at[k - 1], ezr.at[k - 1], e, (x + 4 - k) % 4,
            )
            copy.start()
            summed_early[k - 1] = copy

    for i in range(RING):
        send_pair(i)
        if i >= LAG:
            forward_pair(i - LAG)
        if i == EARLY_AFTER:
            route_early()
    for copy in loads:
        copy.wait()
    hidden(0)
    for i in range(RING - LAG, RING):
        forward_pair(i)
    send_far(0)
    send_near_free(0)
    send_back_early(0)
    hidden(1)
    send_far(1)
    send_far(2)
    send_near_late(0)
    send_back_early(1)
    send_near_free(1)
    send_near_free(2)
    send_near_late(1)
    send_near_late(2)
    send_back(0)

    send_back(1)
    send_back(2)
    sums_early = send_home_early()
    halves_home = []
    for h, (start, last) in enumerate(((0, SPLIT), (SPLIT, WIDTH))):
        for copy in (returned[0] if h == 0 else []) + returned[1 + h]:
            copy.wait_recv()
        mixture = dot_nn(mix_hi[...], back[:, start:last]) + dot_nn(mix_lo[...], back[:, start:last])
        z_out[:, start:last] = mixture.astype(BF16)
        for du in FAR_FIRST:
            copy = remote(
                z_out.at[du * TOK:(du + 1) * TOK, start:last], z_in.at[du, :, start:last],
                s4s.at[h, du - 1], s4r.at[h, du - 1], home_of(du), x,
            )
            copy.start()
            homes.append(copy)
        halves_home.append(mixture[0:TOK, :])
    send_sums_early(sums_early)
    for h, (start, last) in enumerate(((0, SPLIT), (SPLIT, WIDTH))):
        total = halves_home[h]
        for du, copy in zip(FAR_FIRST, homes[7 * h:]):
            copy.wait_recv()
            total = total + z_in[du, :, start:last].astype(F32)
        if h == 0:
            part = total[:, 0:EARLY_BACK]
            out[:, EARLY_BACK:SPLIT] = total[:, EARLY_BACK:SPLIT].astype(BF16)
        else:
            out[:, SPLIT:WIDTH] = total.astype(BF16)
    for k, copy in enumerate(summed_early):
        copy.wait_recv()
        part = part + early_sum[k].astype(F32)
    out[:, 0:EARLY_BACK] = part.astype(BF16)

    early_copies = crossing + gathers_early + routed_early[1:] + returned_early[1:] + homes_early + summed_early
    for copy in gathers + routed[1:] + sum(sent + forwarded + far + near + returned, []) + homes + early_copies:
        copy.wait_send()


def per_device(tokens, routes, router_probs, w_gate, w_up, w_down):
    vmem = pl.BlockSpec(memory_space=pltpu.VMEM)
    hbm = pl.BlockSpec(memory_space=pltpu.HBM)
    dma = pltpu.SemaphoreType.DMA
    return pl.pallas_call(
        kernel,
        out_shape=jax.ShapeDtypeStruct((TOK, WIDTH), BF16),
        in_specs=[hbm] * 6,
        out_specs=vmem,
        scratch_shapes=[
            pltpu.VMEM((TOP, TOK), jnp.int32),
            pltpu.VMEM((TOP, TOK), F32),
            pltpu.VMEM((4, HID, WIDTH), BF16),
            pltpu.VMEM((4, HID, WIDTH), BF16),
            pltpu.VMEM((4, HID, WIDTH), BF16),
            pltpu.VMEM((RING * 128, 4 * EXPERTS), BF16),
            pltpu.VMEM((RING, TOK, 128), BF16),
            pltpu.VMEM((RING * TOK, MSG), BF16),
            pltpu.VMEM((SLOTS, WIDTH), BF16),
            pltpu.VMEM((SLOTS, WIDTH), BF16),
            pltpu.VMEM((3, SLOTS, LATE_OUT), BF16),
            pltpu.VMEM((RING * TOK, SLOTS), BF16),
            pltpu.VMEM((RING * TOK, SLOTS), BF16),
            pltpu.VMEM((SLOTS, HID), BF16),
            pltpu.VMEM((GROUPS, ROWS_G, WIDTH), BF16),
            pltpu.VMEM((2, GROUPS, HALF_G, WIDTH), BF16),
            pltpu.VMEM((2, GROUPS, HALF_G, WIDTH), F32),
            pltpu.VMEM((2, GROUPS, ROWS_G, WIDTH), BF16),
            pltpu.VMEM((2, GROUPS, ROWS_G, WIDTH), BF16),
            pltpu.VMEM((SLOTS, WIDTH), BF16),
            pltpu.VMEM((SLOTS, WIDTH), BF16),
            pltpu.VMEM((RING * TOK, WIDTH), BF16),
            pltpu.VMEM((RING, TOK, WIDTH), BF16),
            pltpu.VMEM((RING * TOK, 3 * EARLY_OUT), BF16),
            pltpu.VMEM((SLOTS, 3 * EARLY_OUT), BF16),
            pltpu.VMEM((SLOTS, 3 * EARLY_OUT), BF16),
            pltpu.VMEM((SLOTS, 3 * EARLY_BACK), BF16),
            pltpu.VMEM((SLOTS, 3 * EARLY_BACK), BF16),
            pltpu.VMEM((RING * TOK, 3 * EARLY_BACK), BF16),
            pltpu.VMEM((RING, TOK, 3 * EARLY_BACK), BF16),
            pltpu.VMEM((TOK, 3 * EARLY_BACK), BF16),
            pltpu.VMEM((3, TOK, EARLY_BACK), BF16),
            dma((3,)),
            dma((12,)),
            dma((7,)), dma((7,)),
            dma((7,)), dma((7,)),
            dma((16,)), dma((16,)),
            dma((2, RING)), dma((2, RING)),
            dma((2, RING)), dma((2, RING)),
            dma((2, len(PARTS))), dma((2, len(PARTS))),
            dma((2, len(PARTS), 2)), dma((2, len(PARTS), 2)),
            dma((len(PARTS), 16)), dma((len(PARTS), 16)),
            dma((2, 7)), dma((2, 7)),
            dma((3,)), dma((3,)),
            dma((7,)), dma((7,)),
            dma((16,)), dma((16,)),
            dma((16,)), dma((16,)),
            dma((7,)), dma((7,)),
            dma((3,)), dma((3,)),
        ],
        compiler_params=pltpu.CompilerParams(
            collective_id=0, has_side_effects=True, vmem_limit_bytes=40 * 1024 * 1024
        ),
    )(*(
        pltpu.with_memory_space_constraint(a, pltpu.HBM)
        for a in (tokens, routes.T, router_probs.T, w_gate, w_up, w_down)
    ))


def solution(mesh):
    in_specs = (
        P("expert", "pair"),
        P("expert", None),
        P("expert", None),
        P("expert", "pair", None),
        P("expert", "pair", None),
        P("expert", "pair", None),
    )
    out_specs = P("expert", "pair")
    return jax.shard_map(
        per_device, mesh=mesh, in_specs=in_specs, out_specs=out_specs, check_vma=False
    )
```
